512 devices in a mesh: tm: 16 (over y_hi, z), gz: 32 (over y_lo, x, core).
Axes of the slice: x: 4, y: 8 (y_hi: 2, y_lo: 4; y = y_hi * 4 + y_lo), z: 8, core: 2. Of those that a mesh axis runs over, the one named last changes fastest.
Arguments:
- starts: float32 [16, 128, 128, 128], P('tm', 'gz'), may hold values from -6 to 6
- materials: int32 [128, 128, 128], P('gz'), may hold values from 0 to 2
- conductivity: float32 [3], replicated, may hold values from 0.4 to 2.5
- pre_factor: float32 [3], replicated, may hold values from 0.2 to 1
- activation: float32 [3], replicated, may hold values from 0.5 to 1.5
Outputs:
- next_starts: float32 [16, 128, 128, 128], P('tm', 'gz')
The draws below stay inside these ranges and needn't reach their ends.
Inputs may be any that keep to these rules, and one draw needn't show every extreme that they name: `materials`: material ids: 0 cell, 1 coolant, 2 casing.
All inputs are finite; a program needn't handle non-finite values.
Results may differ from the reference program's by a relative error of at most 0.0001.
Values sent between devices are 32-bit elements; how exact they have to be, the bound alone decides.
A program may use at most 128 MiB of HBM per device.

```python
import math
import jax
import jax.numpy as jnp
from jax import lax

NX = 128
NY = 128
FSTEPS = 4
CSTEPS = 1
MATERIALS = 3
NZ = 128
SLICES = 16


def place_ends(values, key, low, top_value):
    shape = values.shape
    index_at = [jax.random.randint(jax.random.fold_in(key, axis), (), 0, shape[axis]) for axis in range(len(shape))]
    values = values.at[tuple(index_at)].set(low)
    longest = shape.index(max(shape))
    index_at[longest] = (index_at[longest] + 1) % shape[longest]
    return values.at[tuple(index_at)].set(top_value)


def block_levels(rng, shape, shards, low, high):
    level, own = 1.0, jax.random.fold_in(rng, 6)
    for axis_at, blocks in shards:
        heights = jnp.exp(jax.random.uniform(jax.random.fold_in(own, axis_at), (blocks,), jnp.float32, low / len(shards), high / len(shards)))
        level = level * jnp.repeat(heights, shape[axis_at] // blocks).reshape([-1 if axis == axis_at else 1 for axis in range(len(shape))])
    return level


def gaussian(rng, dims, spread, bound, cuts=(), dtype=jnp.bfloat16):
    values = jax.random.normal(rng, dims, jnp.float32) * spread
    if len(cuts) > 0:
        values = block_levels(rng, dims, cuts, -0.22, 0.18) * values
    return jnp.clip(values, min=-bound, max=bound).astype(dtype)


def setup_inputs(seed: int = 0) -> dict:
    splits = jax.random.split(jax.random.key(seed), 6)
    starts = gaussian(splits[0], (SLICES, NZ, NX, NY), 1.0, 6.0, ((0, 16), (1, 32)), jnp.float32)
    materials = place_ends(jax.random.randint(splits[1], (NZ, NX, NY), 0, 3), jax.random.fold_in(splits[1], 1), 0, 2).astype(jnp.int32)
    conductivity = jnp.clip(jnp.exp(jax.random.uniform(splits[2], (MATERIALS,), jnp.float32, math.log(0.4), math.log(2.5))), 0.4, 2.5)
    pre_factor = jnp.clip(jax.random.uniform(splits[3], (MATERIALS,), jnp.float32, 0.2, 1.0), 0.2, 1.0)
    activation = jnp.clip(jax.random.uniform(splits[4], (MATERIALS,), jnp.float32, 0.5, 1.5), 0.5, 1.5)
    return dict(starts=starts, materials=materials, conductivity=conductivity, pre_factor=pre_factor, activation=activation)


step_size = 0.06


def lookup(identity, table):
    total = jnp.zeros(identity.shape, jnp.float32)
    for index in range(3):
        total = total + jnp.where(identity == index, table[index], jnp.float32(0.0))
    return total


def heat_step(padded, conduct, source_pre, source_act, step_dt, inv_area):
    centre = padded[1:-1, 1:-1, 1:-1]
    cond_centre = conduct[1:-1, 1:-1, 1:-1]
    windows = [
        (slice(2, None), slice(1, -1), slice(1, -1)),
        (slice(None, -2), slice(1, -1), slice(1, -1)),
        (slice(1, -1), slice(2, None), slice(1, -1)),
        (slice(1, -1), slice(None, -2), slice(1, -1)),
        (slice(1, -1), slice(1, -1), slice(2, None)),
        (slice(1, -1), slice(1, -1), slice(None, -2)),
    ]
    total = jnp.zeros(centre.shape, jnp.float32)
    for window in windows:
        total = total + 0.5 * (cond_centre + conduct[window]) * (padded[window] - centre)
    release = source_pre * jnp.exp(source_act * centre / (1.0 + jnp.abs(centre)))
    return centre + step_dt * (inv_area * total + release)


def down(field):
    depth, width, height = field.shape
    return field.reshape(depth // 4, 4, width // 4, 4, height // 4, 4).mean(axis=(1, 3, 5))


def up(field):
    return jnp.repeat(jnp.repeat(jnp.repeat(field, 4, 0), 4, 1), 4, 2)


def reference(starts, materials, conductivity, pre_factor, activation):
    cond_pad = lookup(jnp.pad(materials, 1), conductivity)
    fine_pre = lookup(materials, pre_factor)
    fine_act = lookup(materials, activation)
    coarse_cond = jnp.pad(down(lookup(materials, conductivity)), 1, constant_values=conductivity[0])
    coarse_pre = down(fine_pre)
    coarse_act = down(fine_act)
    coarse_dt = step_size * FSTEPS / CSTEPS

    def fine_run(field):
        for step in range(FSTEPS):
            field = heat_step(jnp.pad(field, 1), cond_pad, fine_pre, fine_act, step_size, 1.0)
        return field

    def coarse_run(state):
        for step in range(CSTEPS):
            state = heat_step(jnp.pad(state, 1), coarse_cond, coarse_pre, coarse_act, coarse_dt, 1.0 / 16.0)
        return state

    def correction(field):
        return fine_run(field) - up(coarse_run(down(field)))

    diffs = lax.map(correction, starts)

    def chain(state, diff):
        latest = coarse_run(state)
        return latest + down(diff), up(latest) + diff

    final_state, advanced = lax.scan(chain, down(starts[0]), diffs[:-1])
    return jnp.concatenate([starts[:1], advanced], 0)
```

```python
import functools

import jax
import jax.numpy as jnp
from jax import lax
from jax.experimental import pallas as pl
from jax.experimental.pallas import tpu as pltpu
from jax.sharding import PartitionSpec as P

FSTEPS = 4
CSTEPS = 1
STEP = 0.06
MESH = pl.DeviceIdType.MESH
F32 = jnp.float32
NG = 32
NT = 16


def dot(a, b):
    return jnp.dot(a, b, precision=lax.Precision.HIGHEST, preferred_element_type=F32)


def iota(shape, dim):
    return lax.broadcasted_iota(jnp.int32, shape, dim)


def ones_where(mask):
    return jnp.where(mask, F32(1.0), F32(0.0))


def pool_mats():
    cols = ones_where(iota((128, 128), 0) // 4 == iota((128, 128), 1) % 32)
    rows = ones_where(iota((32, 128), 0) == iota((32, 128), 1) // 4)
    return cols, rows


def pool(total, mats):
    cols, rows = mats
    u = dot(rows, dot(total, cols))
    group = iota((8, 128), 1) // 32
    out = jnp.zeros((8, 128), F32)
    for g in range(4):
        out = out + jnp.where(group == g, u[8 * g : 8 * g + 8], F32(0.0))
    return out * F32(1.0 / 64.0)


def unpool(coarse):
    group = iota((8, 128), 1) // 32
    u = jnp.concatenate([jnp.where(group == g, coarse, F32(0.0)) for g in range(4)], axis=0)
    rows_t = ones_where(iota((128, 32), 0) // 4 == iota((128, 32), 1))
    cols_t = ones_where(iota((128, 128), 0) % 32 == iota((128, 128), 1) // 4)
    return dot(dot(rows_t, u), cols_t)


def release(v, hp, act):
    return hp * jnp.exp(act * v / (1.0 + jnp.abs(v)))


def lookup(ids, table):
    return jnp.where(ids == 0, table[0], jnp.where(ids == 1, table[1], table[2]))


def coarse_shifts(v):
    row = iota(v.shape, 1)
    right = pltpu.roll(v, 127, 2)
    left = pltpu.roll(v, 1, 2)
    up = pltpu.roll(v, 7, 1)
    up = jnp.where(row == 7, pltpu.roll(up, 96, 2), up)
    down = pltpu.roll(v, 1, 1)
    down = jnp.where(row == 0, pltpu.roll(down, 32, 2), down)
    return right, left, up, down


def coarse_coefs(k, p, outside, inside):
    scale = F32(STEP * FSTEPS / CSTEPS / 16.0 * 0.5)
    n = k.shape[0] - 2
    mid = k[1:-1]
    lane = iota(mid.shape, 2)
    row = iota(mid.shape, 1)
    right, left, up, down = coarse_shifts(mid)
    edges = (
        (right, lane % 32 == 31),
        (left, lane % 32 == 0),
        (up, (row == 7) & (lane >= 96)),
        (down, (row == 0) & (lane < 32)),
    )
    keep = F32(1.0)
    sides = []
    for other, edge in edges:
        face = scale * (mid + jnp.where(edge, outside, other))
        keep = keep - face
        sides.append(jnp.where(edge, F32(0.0), face))
    faces = scale * (k[1:] + k[:-1])
    keep = keep - faces[1:] - faces[:-1]
    both = [jnp.where(inside[i] & inside[i + 1], faces[i : i + 1], F32(0.0)) for i in range(n + 1)]
    vertical = jnp.concatenate(both, axis=0)
    return sides, vertical, keep, F32(STEP * FSTEPS / CSTEPS) * p


def coarse_step(c, sides, below, above, keep, hp, act):
    mid = c[1:-1]
    out = mid * keep + below * c[:-2] + above * c[2:]
    for other, face in zip(coarse_shifts(mid), sides):
        out = out + face * other
    return out + release(mid, hp, act)


def kernel(
    starts,
    materials,
    cond,
    pre,
    act,
    out,
    fa,
    fb,
    ids,
    kbuf,
    kz,
    kxr,
    kxl,
    kyu,
    kyd,
    keep,
    hp,
    actb,
    fprev,
    oldv,
    gbuf,
    dbuf,
    c8,
    gs,
    cz,
    cside,
    ckeep,
    chp,
    local_sem,
    slab_s,
    slab_r,
    c0_s,
    c0_r,
    gc_s,
    gc_r,
    dt_s,
    dt_r,
    dg_s,
    dg_r,
    cr_s,
    cr_r,
    f_s,
    f_r,
    know,
):
    tm = lax.axis_index("tm")
    gz = lax.axis_index("gz")
    zi = lax.rem(tm, 8)
    hi = tm // 8
    yy = hi * 4 + gz // 8
    rest = lax.rem(gz, 8)

    def ring(k):
        return (hi * 8 + lax.rem(zi + (k % 8), 8), gz)

    def ygo(k):
        y = lax.rem(yy + (k % 8), 8)
        return ((y // 4) * 8 + zi, lax.rem(y, 4) * 8 + rest)

    def has(j):
        return (gz + j >= 0) & (gz + j < NG)

    def remote(src, dst, send, recv, where):
        return pltpu.make_async_remote_copy(
            src_ref=src, dst_ref=dst, send_sem=send, recv_sem=recv, device_id=where, device_id_type=MESH
        )

    def tell(sem, where):
        pl.semaphore_signal(sem, 1, device_id=where, device_id_type=MESH)

    def tell_layers(sem, dist):
        for j in (-dist, dist):

            @pl.when(has(j))
            def _():
                tell(sem, (tm, gz + j))

    def hear(sem, dist, more):
        pl.semaphore_wait(sem, has(-dist).astype(jnp.int32) + has(dist).astype(jnp.int32) + more)

    c0, is_b = cond[0], hi == 1

    own_f = pltpu.make_async_copy(starts, fa.at[pl.ds(4, 4)], local_sem.at[0])
    own_m = pltpu.make_async_copy(materials, ids.at[pl.ds(4, 4)], local_sem.at[1])
    own_m.start()
    own_f.start()
    for j, at in ((-1, 0), (1, 8)):

        @pl.when(jnp.logical_not(has(j)))
        def _():
            fa[pl.ds(at, 4)] = jnp.zeros((4, 128, 128), F32)
            ids[pl.ds(at, 4)] = jnp.zeros((4, 128, 128), jnp.int32)

    gbuf[...] = jnp.zeros(gbuf.shape, F32)
    gbuf[:, 0] = jnp.full((17, 8, 128), c0, F32)
    dbuf[...] = jnp.zeros(dbuf.shape, F32)
    c8[...] = jnp.zeros(c8.shape, F32)

    barrier = pltpu.get_barrier_semaphore()
    tell_layers(barrier, 1)
    for k in (1, -1):
        tell(barrier, ring(k))
        tell(barrier, ygo(k))
    hear(barrier, 1, 4)

    def slab(j, n, what):
        side = 0 if j > 0 else 1
        here = 3 - n if j > 0 else n
        there = here if j > 0 else 8 + here
        src, dst = (starts, fa) if what == 0 else (materials, ids)
        return remote(
            src.at[here], dst.at[there], slab_s.at[side, n, what], slab_r.at[side, n, what], (tm, gz + j)
        )

    for n in range(4):
        for j in (1, -1):

            @pl.when(has(j))
            def _():
                slab(j, n, 1).start()
                slab(j, n, 0).start()

    tell_layers(know.at[0], 1)
    for k in (1, -1):
        tell(know.at[0], ring(k))
        tell(know.at[0], ygo(k))

    mats = pool_mats()
    own_m.wait()
    totals = [jnp.zeros((128, 128), F32) for _ in range(3)]
    for n in range(4):
        layer = ids[4 + n]
        totals = [t + lookup(layer, table) for t, table in zip(totals, (cond, pre, act))]
    for i in range(3):
        gbuf[8, i] = pool(totals[i], mats)
    own_f.wait()
    own_coarse = pool(fa[4] + fa[5] + fa[6] + fa[7], mats)

    @pl.when((tm == 0) | is_b)
    def _():
        gbuf[8, 3] = jnp.where(is_b, F32(0.0), own_coarse)

    out[...] = fa[pl.ds(4, 4)]

    hear(know.at[0], 1, 4)
    tell_layers(know.at[1], 2)
    for k in (2, -2):
        tell(know.at[1], ring(k))
        tell(know.at[1], ygo(k))
    hear(know.at[1], 2, 4)
    tell_layers(know.at[2], 4)
    tell(know.at[2], ygo(4))

    def c0_copy(n):
        return remote(gbuf.at[8, 3], gbuf.at[8, 3], c0_s.at[n - 1], c0_r, (n, gz))

    @pl.when(tm == 0)
    def _():
        for n in range(1, 8):
            c0_copy(n).start()

    for n in range(4):
        for j in (1, -1):

            @pl.when(has(-j))
            def _():
                slab(j, n, 1).wait_recv()
                slab(j, n, 0).wait_recv()

    lane = iota((128, 128), 1)
    row = iota((128, 128), 0)

    def inside_fine(layer):
        return jnp.logical_not(((layer < 4) & (gz == 0)) | ((layer >= 8) & (gz == NG - 1)))

    def conduct(layer, _):
        kbuf[layer] = lookup(ids[layer], cond)
        return 0

    lax.fori_loop(0, 12, conduct, 0)
    half = F32(0.5 * STEP)

    def fine_coef(layer, _):
        k = kbuf[layer]
        inside = inside_fine(layer)
        above = half * (k + kbuf[layer + 1])
        below = half * (k + kbuf[layer - 1])
        rest_of = 1.0 - above - below
        for other, edge, ref in (
            (pltpu.roll(k, 127, 1), lane == 127, kxr),
            (pltpu.roll(k, 1, 1), lane == 0, kxl),
            (pltpu.roll(k, 127, 0), row == 127, kyu),
            (pltpu.roll(k, 1, 0), row == 0, kyd),
        ):
            face = half * (k + jnp.where(edge, c0, other))
            rest_of = rest_of - face
            ref[layer] = jnp.where(edge, F32(0.0), face)
        keep[layer] = rest_of
        kz[layer] = jnp.where(inside & inside_fine(layer + 1), above, F32(0.0))

        @pl.when(layer == 1)
        def _():
            kz[0] = jnp.where(inside & inside_fine(layer - 1), below, F32(0.0))

        ident = ids[layer]
        hp[layer] = jnp.where(inside, F32(STEP) * lookup(ident, pre), F32(0.0))
        actb[layer] = lookup(ident, act)
        return 0

    lax.fori_loop(1, 11, fine_coef, 0)

    k_near = jnp.stack(
        [
            pool(kbuf[0] + kbuf[1] + kbuf[2] + kbuf[3], mats),
            gbuf[8, 0],
            pool(kbuf[8] + kbuf[9] + kbuf[10] + kbuf[11], mats),
        ]
    )
    near = jnp.stack(
        [
            pool(fa[0] + fa[1] + fa[2] + fa[3], mats),
            own_coarse,
            pool(fa[8] + fa[9] + fa[10] + fa[11], mats),
        ]
    )
    sides, vertical, kept, heat = coarse_coefs(k_near, gbuf[8, 1][None], c0, [has(-1), has(0), has(1)])
    old = coarse_step(near, sides, vertical[:1], vertical[1:], kept, heat, gbuf[8, 2][None])[0]
    oldv[0] = old

    for step in range(FSTEPS):
        src, dst = (fa, fb) if step % 2 == 0 else (fb, fa)

        def fine_step(layer, _):
            v = src[layer]
            new = v * keep[layer] + kz[layer - 1] * src[layer - 1] + kz[layer] * src[layer + 1]
            new = new + kxr[layer] * pltpu.roll(v, 127, 1) + kxl[layer] * pltpu.roll(v, 1, 1)
            new = new + kyu[layer] * pltpu.roll(v, 127, 0) + kyd[layer] * pltpu.roll(v, 1, 0)
            dst[layer] = new + release(v, hp[layer], actb[layer])
            return 0

        lax.fori_loop(step + 1, 11 - step, fine_step, 0)
    d_own = pool(fa[4] + fa[5] + fa[6] + fa[7], mats) - old
    dbuf[7, zi] = d_own

    def dt_copy(k):
        return remote(dbuf.at[7, zi], dbuf.at[7, zi], dt_s.at[k - 1], dt_r.at[k - 1], ring(k))

    for k in range(1, 8):
        dt_copy(k).start()

    hear(know.at[2], 4, 1)
    tell(know.at[3], ygo(4))

    def pass_fine():
        return remote(fa.at[pl.ds(4, 4)], fprev, f_s.at[0], f_r.at[0], (tm + 1, gz))

    def pass_old():
        return remote(oldv.at[0], oldv.at[1], f_s.at[1], f_r.at[1], (tm + 1, gz))

    @pl.when(tm < NT - 1)
    def _():
        pass_old().start()
        pass_fine().start()

    @pl.when((tm > 0) & (tm < 8))
    def _():
        c0_copy(1).wait_recv()

    def gc_copy(j):
        i = j + 8 if j < 0 else j + 7
        return remote(gbuf.at[8], gbuf.at[8 - j], gc_s.at[i], gc_r.at[i], (tm, gz + j))

    around = [j for d in range(1, 9) for j in (d, -d)]
    for j in around:

        @pl.when(has(j))
        def _():
            gc_copy(j).start()

    for k in range(1, 8):
        dt_copy(k).wait_recv()

    def dg_copy(j):
        i = j + 7 if j < 0 else j + 6
        n = 8 - abs(j)
        return remote(
            dbuf.at[7, pl.ds(0, n)], dbuf.at[7 - j, pl.ds(0, n)], dg_s.at[i], dg_r.at[i], (tm, gz + j)
        )

    for j in around[:14]:

        @pl.when(has(j))
        def _():
            dg_copy(j).start()

    for j in around:

        @pl.when(has(-j))
        def _():
            gc_copy(j).wait_recv()

    sides, vertical, kept, heat = coarse_coefs(gbuf[:, 0], gbuf[1:16, 1], c0, [has(j) for j in range(-8, 9)])
    for i in range(4):
        cside[i] = sides[i]
    cz[...] = vertical
    ckeep[...] = kept
    chp[...] = heat

    for j in around[:14]:

        @pl.when(has(-j))
        def _():
            dg_copy(j).wait_recv()

    def cr_copy(j):
        return remote(gs.at[9], c8.at[8 - j], cr_s.at[j + 7], cr_r.at[j + 7], (tm + 8, gz + j))

    def g8_copy():
        return remote(gs.at[8], gs.at[0], cr_s.at[15], cr_r.at[15], (tm + 8, gz))

    for j in range(-7, 8):

        @pl.when(is_b & has(-j) & (zi >= abs(j)))
        def _():
            cr_copy(j).wait_recv()

    @pl.when(is_b)
    def _():
        g8_copy().wait_recv()

    state = jnp.where(is_b, c8[...], gbuf[:, 3])
    for s in range(1, 9):
        n = 17 - 2 * s
        lo = s - 1
        latest = coarse_step(
            state,
            [cside[i, pl.ds(lo, n)] for i in range(4)],
            cz[pl.ds(lo, n)],
            cz[pl.ds(lo + 1, n)],
            ckeep[pl.ds(lo, n)],
            chp[pl.ds(lo, n)],
            gbuf[pl.ds(lo + 1, n), 2],
        )
        gs[s] = latest[8 - s]
        state = latest + dbuf[pl.ds(lo, n), s - 1]
    gs[9] = state[0]

    is_a = jnp.logical_not(is_b)
    pl.semaphore_wait(know.at[3], 1)
    for j in range(-7, 8):

        @pl.when(is_a & has(j) & (zi >= abs(j)))
        def _():
            cr_copy(j).start()

    @pl.when(is_a)
    def _():
        g8_copy().start()

    @pl.when(tm > 0)
    def _():
        pass_old().wait_recv()
        pass_fine().wait_recv()
        fine = unpool(gs[zi] - oldv[1])
        for n in range(4):
            out[n] = fprev[n] + fine

    for n in range(4):
        for j in (1, -1):

            @pl.when(has(j))
            def _():
                slab(j, n, 1).wait_send()
                slab(j, n, 0).wait_send()

    @pl.when(tm == 0)
    def _():
        for n in range(1, 8):
            c0_copy(n).wait_send()

    for k in range(1, 8):
        dt_copy(k).wait_send()

    @pl.when(tm < NT - 1)
    def _():
        pass_old().wait_send()
        pass_fine().wait_send()

    for j in around:

        @pl.when(has(j))
        def _():
            gc_copy(j).wait_send()

    for j in around[:14]:

        @pl.when(has(j))
        def _():
            dg_copy(j).wait_send()

    for j in range(-7, 8):

        @pl.when(is_a & has(j) & (zi >= abs(j)))
        def _():
            cr_copy(j).wait_send()

    @pl.when(is_a)
    def _():
        g8_copy().wait_send()


def on_device(starts, materials, conductivity, pre_factor, activation):
    vmem, dma = pltpu.VMEM, pltpu.SemaphoreType.DMA
    slabs = vmem((12, 128, 128), F32)
    tile = lambda *lead: vmem(lead + (8, 128), F32)
    result = pl.pallas_call(
        kernel,
        name="parareal",
        out_shape=jax.ShapeDtypeStruct((4, 128, 128), F32),
        in_specs=[pl.BlockSpec(memory_space=pl.ANY)] * 2 + [pl.BlockSpec(memory_space=pltpu.SMEM)] * 3,
        out_specs=pl.BlockSpec(memory_space=pltpu.VMEM),
        scratch_shapes=[
            slabs,
            slabs,
            vmem((12, 128, 128), jnp.int32),
            *([slabs] * 9),
            vmem((4, 128, 128), F32),
            tile(2),
            tile(17, 4),
            tile(15, 8),
            tile(17),
            tile(10),
            tile(16),
            tile(4, 15),
            tile(15),
            tile(15),
            dma((2,)),
            dma((2, 4, 2)),
            dma((2, 4, 2)),
            dma((7,)),
            dma(()),
            dma((16,)),
            dma((16,)),
            dma((7,)),
            dma((7,)),
            dma((14,)),
            dma((14,)),
            dma((16,)),
            dma((16,)),
            dma((2,)),
            dma((2,)),
            pltpu.SemaphoreType.REGULAR((4,)),
        ],
        compiler_params=pltpu.CompilerParams(
            collective_id=0, has_side_effects=True, vmem_limit_bytes=40 * 2**20
        ),
        cost_estimate=pl.CostEstimate(flops=50_000_000, bytes_accessed=2_000_000, transcendentals=500_000),
    )(starts[0], materials, conductivity, pre_factor, activation)
    return result[None]


def solution(mesh):
    return jax.shard_map(
        on_device,
        mesh=mesh,
        in_specs=(P("tm", "gz", None, None), P("gz", None, None), P(), P(), P()),
        out_specs=P("tm", "gz", None, None),
        check_vma=False,
    )
```

```python
import functools

import jax
import jax.numpy as jnp
from jax import lax
from jax.experimental import pallas as pl
from jax.experimental.pallas import tpu as pltpu
from jax.sharding import PartitionSpec as P

FSTEPS = 4
CSTEPS = 1
STEP = 0.06
MESH = pl.DeviceIdType.MESH
F32 = jnp.float32
NG = 32
NT = 16


def dot(a, b):
    return jnp.dot(a, b, precision=lax.Precision.HIGHEST, preferred_element_type=F32)


def iota(shape, dim):
    return lax.broadcasted_iota(jnp.int32, shape, dim)


def ones_where(mask):
    return jnp.where(mask, F32(1.0), F32(0.0))


def pool(totals):
    n = len(totals)
    cols = ones_where(iota((128, 128), 0) // 4 == iota((128, 128), 1) % 32)
    rows = ones_where(iota((32, 128), 0) == iota((32, 128), 1) // 4)
    wide = dot(rows, jnp.concatenate(totals, axis=1))
    tall = dot(jnp.concatenate([wide[:, 128 * i : 128 * i + 128] for i in range(n)], axis=0), cols)
    group = iota((8, 128), 1) // 32
    outs = []
    for i in range(n):
        out = jnp.zeros((8, 128), F32)
        for g in range(4):
            at = 32 * i + 8 * g
            out = out + jnp.where(group == g, tall[at : at + 8], F32(0.0))
        outs.append(out * F32(1.0 / 64.0))
    return outs


def unpool(coarse):
    group = iota((8, 128), 1) // 32
    u = jnp.concatenate([jnp.where(group == g, coarse, F32(0.0)) for g in range(4)], axis=0)
    rows_t = ones_where(iota((128, 32), 0) // 4 == iota((128, 32), 1))
    cols_t = ones_where(iota((128, 128), 0) % 32 == iota((128, 128), 1) // 4)
    return dot(rows_t, dot(u, cols_t))


def release(v, hp, act):
    return hp * jnp.exp(act * v / (1.0 + jnp.abs(v)))


def lookup(ids, table):
    return jnp.where(ids == 0, table[0], jnp.where(ids == 1, table[1], table[2]))


def coarse_shifts(v):
    row = iota(v.shape, 1)
    right = pltpu.roll(v, 127, 2)
    left = pltpu.roll(v, 1, 2)
    up = pltpu.roll(v, 7, 1)
    up = jnp.where(row == 7, pltpu.roll(up, 96, 2), up)
    down = pltpu.roll(v, 1, 1)
    down = jnp.where(row == 0, pltpu.roll(down, 32, 2), down)
    return right, left, up, down


def coarse_coefs(k, p, outside, inside):
    scale = F32(STEP * FSTEPS / CSTEPS / 16.0 * 0.5)
    n = k.shape[0] - 2
    mid = k[1:-1]
    lane = iota(mid.shape, 2)
    row = iota(mid.shape, 1)
    right, left, up, down = coarse_shifts(mid)
    edges = (
        (right, lane % 32 == 31),
        (left, lane % 32 == 0),
        (up, (row == 7) & (lane >= 96)),
        (down, (row == 0) & (lane < 32)),
    )
    keep = F32(1.0)
    sides = []
    for other, edge in edges:
        face = scale * (mid + jnp.where(edge, outside, other))
        keep = keep - face
        sides.append(jnp.where(edge, F32(0.0), face))
    faces = scale * (k[1:] + k[:-1])
    keep = keep - faces[1:] - faces[:-1]
    both = [jnp.where(inside[i] & inside[i + 1], faces[i : i + 1], F32(0.0)) for i in range(n + 1)]
    vertical = jnp.concatenate(both, axis=0)
    return sides, vertical, keep, F32(STEP * FSTEPS / CSTEPS) * p


def coarse_step(c, sides, below, above, keep, hp, act):
    mid = c[1:-1]
    out = mid * keep + below * c[:-2] + above * c[2:]
    for other, face in zip(coarse_shifts(mid), sides):
        out = out + face * other
    return out + release(mid, hp, act)


def kernel(
    starts,
    materials,
    cond,
    pre,
    act,
    out,
    fab,
    ids,
    kbuf,
    kz,
    kxr,
    kxl,
    kyu,
    kyd,
    keep,
    hp,
    actb,
    fprev,
    relay,
    oldv,
    near,
    gbuf,
    dbuf,
    c8,
    state,
    gs,
    cz,
    cside,
    ckeep,
    chp,
    local_sem,
    near_s,
    near_r,
    slab_s,
    slab_r,
    c0_s,
    c0_r,
    gc_s,
    gc_r,
    dt_s,
    dt_r,
    dg_s,
    dg_r,
    dl_s,
    dl_r,
    cr_s,
    cr_r,
    f_s,
    f_r,
    rl_s,
    rl_r,
    know,
):
    tm = lax.axis_index("tm")
    gz = lax.axis_index("gz")
    zi = lax.rem(tm, 8)
    hi = tm // 8
    yy = hi * 4 + gz // 8
    rest = lax.rem(gz, 8)

    def ring(k):
        return (hi * 8 + lax.rem(zi + (k % 8), 8), gz)

    def ygo(k):
        y = lax.rem(yy + (k % 8), 8)
        return ((y // 4) * 8 + zi, lax.rem(y, 4) * 8 + rest)

    def has(j):
        return (gz + j >= 0) & (gz + j < NG)

    def has_slice(k):
        return (zi + k >= 0) & (zi + k < 8)

    def remote(src, dst, send, recv, where):
        return pltpu.make_async_remote_copy(
            src_ref=src, dst_ref=dst, send_sem=send, recv_sem=recv, device_id=where, device_id_type=MESH
        )

    pending = []

    def send(when, *copies):
        @pl.when(when)
        def _():
            for copy in copies:
                copy().start()

        pending.append((when, copies))

    def finish():
        for when, copies in pending:

            @pl.when(when)
            def _(copies=copies):
                for copy in copies:
                    copy().wait_send()

    def tell_one(sem, where):
        pl.semaphore_signal(sem, 1, device_id=where, device_id_type=MESH)

    def tell(sem, dist):
        for j in (-dist, dist):

            @pl.when(has(j))
            def _():
                tell_one(sem, (tm, gz + j))

            @pl.when(has_slice(j))
            def _():
                tell_one(sem, (tm + j, gz))

        tell_one(sem, ygo(dist))
        if dist < 4:
            tell_one(sem, ygo(-dist))

    def hear(sem, dist):
        n = 1 if dist == 4 else 2
        for j in (-dist, dist):
            n = n + has(j).astype(jnp.int32) + has_slice(j).astype(jnp.int32)
        pl.semaphore_wait(sem, n)

    c0, is_b = cond[0], hi == 1
    is_a = jnp.logical_not(is_b)

    own_f = pltpu.make_async_copy(starts, fab.at[0, pl.ds(4, 4)], local_sem.at[0])
    own_m = pltpu.make_async_copy(materials, ids.at[pl.ds(4, 4)], local_sem.at[1])
    own_m.start()
    own_f.start()
    for j, at in ((-1, 0), (1, 8)):

        @pl.when(jnp.logical_not(has(j)))
        def _():
            fab[0, pl.ds(at, 4)] = jnp.zeros((4, 128, 128), F32)
            ids[pl.ds(at, 4)] = jnp.zeros((4, 128, 128), jnp.int32)

    near[...] = jnp.zeros(near.shape, F32)
    gbuf[...] = jnp.zeros(gbuf.shape, F32)
    gbuf[:, 0] = jnp.full((17, 8, 128), c0, F32)
    dbuf[...] = jnp.zeros(dbuf.shape, F32)
    c8[...] = jnp.zeros(c8.shape, F32)

    barrier = pltpu.get_barrier_semaphore()
    tell(barrier, 1)

    own_m.wait()
    totals = [jnp.zeros((128, 128), F32) for _ in range(3)]
    for n in range(4):
        layer = ids[4 + n]
        totals = [t + lookup(layer, table) for t, table in zip(totals, (cond, pre, act))]
    own_f.wait()
    totals.append(fab[0, 4] + fab[0, 5] + fab[0, 6] + fab[0, 7])
    pooled = pool(totals)
    for i in range(3):
        gbuf[8, i] = pooled[i]
    own_coarse = pooled[3]
    near[1, 0] = pooled[0]
    near[1, 1] = own_coarse

    @pl.when(tm == 0)
    def _():
        dbuf[8, 0] = own_coarse
        out[...] = fab[0, pl.ds(4, 4)]

    hear(barrier, 1)

    def near_copy(j):
        side = 0 if j > 0 else 1
        return remote(near.at[1], near.at[1 - j], near_s.at[side], near_r.at[side], (tm, gz + j))

    def slab(j, n, what):
        side = 0 if j > 0 else 1
        here = 3 - n if j > 0 else n
        there = here if j > 0 else 8 + here
        src = (starts if what == 0 else materials).at[here]
        dst = fab.at[0, there] if what == 0 else ids.at[there]
        return remote(src, dst, slab_s.at[side, n, what], slab_r.at[side, n, what], (tm, gz + j))

    for j in (1, -1):
        send(has(j), functools.partial(near_copy, j))
    for n in range(4):
        for j in (1, -1):
            send(has(j), functools.partial(slab, j, n, 1), functools.partial(slab, j, n, 0))
    tell(know.at[0], 1)

    lane = iota((128, 128), 1)
    row = iota((128, 128), 0)
    half = F32(0.5 * STEP)

    def inside_fine(layer):
        return jnp.logical_not(((layer < 4) & (gz == 0)) | ((layer >= 8) & (gz == NG - 1)))

    def sources(layer):
        ident, inside = ids[layer], inside_fine(layer)
        kbuf[layer] = lookup(ident, cond)
        hp[layer] = jnp.where(inside, F32(STEP) * lookup(ident, pre), F32(0.0))
        actb[layer] = lookup(ident, act)

    def faces(layer):
        k = kbuf[layer]
        inside = inside_fine(layer)
        above = half * (k + kbuf[layer + 1])
        below = half * (k + kbuf[layer - 1])
        rest_of = 1.0 - above - below
        for other, edge, ref in (
            (pltpu.roll(k, 127, 1), lane == 127, kxr),
            (pltpu.roll(k, 1, 1), lane == 0, kxl),
            (pltpu.roll(k, 127, 0), row == 127, kyu),
            (pltpu.roll(k, 1, 0), row == 0, kyd),
        ):
            face = half * (k + jnp.where(edge, c0, other))
            rest_of = rest_of - face
            ref[layer] = jnp.where(edge, F32(0.0), face)
        keep[layer] = rest_of
        kz[layer] = jnp.where(inside & inside_fine(layer + 1), above, F32(0.0))
        kz[layer - 1] = jnp.where(inside & inside_fine(layer - 1), below, F32(0.0))

    def fine_step(layer, at):
        v = fab[at, layer]
        new = v * keep[layer] + kz[layer - 1] * fab[at, layer - 1] + kz[layer] * fab[at, layer + 1]
        new = new + kxr[layer] * pltpu.roll(v, 127, 1) + kxl[layer] * pltpu.roll(v, 1, 1)
        new = new + kyu[layer] * pltpu.roll(v, 127, 0) + kyd[layer] * pltpu.roll(v, 1, 0)
        fab[1 - at, layer] = new + release(v, hp[layer], actb[layer])

    def slab_here(n):
        for j in (1, -1):

            @pl.when(has(-j))
            def _():
                slab(j, n, 1).wait_recv()
                slab(j, n, 0).wait_recv()

    def stage(n):
        sources(3 - n)
        sources(8 + n)
        if n == 0:

            def own_faces(i, _):
                faces(4 + i)
                return 0

            lax.fori_loop(0, 4, own_faces, 0)
        else:
            faces(4 - n)
            faces(7 + n)

        def pair(i, _):
            at = lax.rem(jnp.minimum(i, n), 2)
            fine_step(4 - n + i, at)
            fine_step(7 + n - i, at)
            return 0

        lax.fori_loop(0, n + 2, pair, 0)

    def own_sources(i, _):
        sources(4 + i)
        return 0

    lax.fori_loop(0, 4, own_sources, 0)
    hear(know.at[0], 1)
    tell(know.at[1], 2)
    for j in (1, -1):

        @pl.when(has(-j))
        def _():
            near_copy(j).wait_recv()

    @pl.when(jnp.logical_not(has(-1)))
    def _():
        near[0, 0] = jnp.full((8, 128), c0, F32)

    @pl.when(jnp.logical_not(has(1)))
    def _():
        near[2, 0] = jnp.full((8, 128), c0, F32)

    sides, vertical, kept, heat = coarse_coefs(
        near[:, 0], gbuf[8, 1][None], c0, [has(-1), has(0), has(1)]
    )
    old = coarse_step(near[:, 1], sides, vertical[:1], vertical[1:], kept, heat, gbuf[8, 2][None])[0]
    oldv[0] = old

    hear(know.at[1], 2)
    tell(know.at[2], 4)
    for n in range(3):
        slab_here(n)
        stage(n)
    hear(know.at[2], 4)
    tell_one(know.at[3], ygo(4))
    tell_one(know.at[3], ring(1))
    tell_one(know.at[3], ring(-1))

    def c0_copy(n):
        return remote(dbuf.at[8, 0], dbuf.at[8, 0], c0_s.at[n - 1], c0_r, (n, gz))

    send(tm == 0, *[functools.partial(c0_copy, n) for n in range(1, 8)])
    slab_here(3)

    def gc_copy(j):
        i = j + 8 if j < 0 else j + 7
        return remote(gbuf.at[8], gbuf.at[8 - j], gc_s.at[i], gc_r.at[i], (tm, gz + j))

    around = [j for d in range(1, 9) for j in (d, -d)]
    for j in around:
        send(has(j), functools.partial(gc_copy, j))

    stage(3)
    dbuf[8, zi + 1] = pool([fab[0, 4] + fab[0, 5] + fab[0, 6] + fab[0, 7]])[0] - old

    def dt_copy(k):
        own = dbuf.at[8, zi + 1]
        return remote(own, own, dt_s.at[k - 1], dt_r.at[zi], ring(k))

    send(tm >= 0, *[functools.partial(dt_copy, k) for k in (4, 3, 5, 2, 6, 1, 7)])

    def dt_here(first, last):
        for at in range(first, last):

            @pl.when(zi != at)
            def _():
                that = dbuf.at[8, at + 1]
                remote(that, that, dt_s.at[0], dt_r.at[at], ring(1)).wait_recv()

    @pl.when(tm == 7)
    def _():
        pl.semaphore_wait(know.at[3], 3)

    def pass_old():
        return remote(oldv.at[0], oldv.at[1], f_s.at[4], f_r.at[4], (tm + 1, gz))

    def pass_fine(n):
        return remote(fab.at[0, 4 + n], fprev.at[n], f_s.at[n], f_r.at[n], (tm + 1, gz))

    def to_relay(n):
        return remote(fab.at[0, 4 + n], relay, rl_s.at[n], rl_r, (n + 3, gz))

    def from_relay(n):
        return remote(relay, fprev.at[n], rl_s.at[0], f_r.at[n], (8, gz))

    send(tm == 7, *[functools.partial(to_relay, n) for n in range(1, 4)], functools.partial(pass_fine, 0), pass_old)

    def dg_copy(j):
        i = j + 8 if j < 0 else j + 7
        some = pl.ds(0, min(5, 9 - abs(j)))
        return remote(dbuf.at[8, some], dbuf.at[8 - j, some], dg_s.at[i], dg_r.at[i], (tm, gz + j))

    def dl_copy(j):
        i = j + 3 if j < 0 else j + 2
        some = pl.ds(5, 4 - abs(j))
        return remote(dbuf.at[8, some], dbuf.at[8 - j, some], dl_s.at[i], dl_r.at[i], (tm, gz + j))

    @pl.when((tm > 0) & (tm < 8))
    def _():
        c0_copy(1).wait_recv()

    dt_here(0, 4)
    for j in around[::-1]:
        send(has(j), functools.partial(dg_copy, j))
    dt_here(4, 7)
    for j in around[:6][::-1]:
        send(has(j), functools.partial(dl_copy, j))
    for n in range(1, 4):

        @pl.when(tm == n + 3)
        def _():
            to_relay(n).wait_recv()

        send(tm == n + 3, functools.partial(from_relay, n))
    send((tm < NT - 1) & (tm != 7), pass_old, *[functools.partial(pass_fine, n) for n in range(4)])

    for j in around:

        @pl.when(has(-j))
        def _():
            gc_copy(j).wait_recv()

    sides, vertical, kept, heat = coarse_coefs(gbuf[:, 0], gbuf[1:16, 1], c0, [has(j) for j in range(-8, 9)])
    for i in range(4):
        cside[i] = sides[i]
    cz[...] = vertical
    ckeep[...] = kept
    chp[...] = heat

    def cr_copy(j):
        return remote(gs.at[9], c8.at[8 - j], cr_s.at[j + 7], cr_r.at[j + 7], (tm + 8, gz + j))

    def g8_copy():
        return remote(gs.at[8], gs.at[0], cr_s.at[15], cr_r.at[15], (8, gz))

    for j in around:

        @pl.when(has(-j))
        def _():
            dg_copy(j).wait_recv()

    for j in range(-7, 8):

        @pl.when(is_b & has(-j) & (zi >= abs(j)))
        def _():
            cr_copy(j).wait_recv()

    state[...] = jnp.where(is_b, c8[...], dbuf[:, 0])
    for s in range(1, 9):
        if s == 5:
            for j in around[:6]:

                @pl.when(has(-j))
                def _():
                    dl_copy(j).wait_recv()

        if s == 8:
            dt_here(7, 8)

        @pl.when(is_a | (zi >= s))
        def _():
            n = 17 - 2 * s
            lo = s - 1
            latest = coarse_step(
                state[pl.ds(lo, n + 2)],
                [cside[i, pl.ds(lo, n)] for i in range(4)],
                cz[pl.ds(lo, n)],
                cz[pl.ds(lo + 1, n)],
                ckeep[pl.ds(lo, n)],
                chp[pl.ds(lo, n)],
                gbuf[pl.ds(s, n), 2],
            )
            gs[s] = latest[8 - s]
            state[pl.ds(s, n)] = latest + dbuf[pl.ds(s, n), s]

    @pl.when(is_a)
    def _():
        gs[9] = state[8]

    @pl.when(tm != 7)
    def _():
        pl.semaphore_wait(know.at[3], 3)

    send(tm == 0, g8_copy)
    for j in sorted(range(-7, 8), key=lambda j: -abs(j)):
        send((tm < 8) & (zi >= abs(j)) & has(j), functools.partial(cr_copy, j))

    @pl.when(tm == 8)
    def _():
        g8_copy().wait_recv()

    @pl.when(tm > 0)
    def _():
        pass_old().wait_recv()
        for n in range(4):
            pass_fine(n).wait_recv()
        fine = unpool(gs[zi] - oldv[1])
        for n in range(4):
            out[n] = fprev[n] + fine

    finish()


def on_device(starts, materials, conductivity, pre_factor, activation):
    vmem, dma = pltpu.VMEM, pltpu.SemaphoreType.DMA
    slabs = vmem((12, 128, 128), F32)
    tile = lambda *lead: vmem(lead + (8, 128), F32)
    held = lambda x: pltpu.with_memory_space_constraint(x, pltpu.HBM)
    result = pl.pallas_call(
        kernel,
        name="parareal",
        out_shape=jax.ShapeDtypeStruct((4, 128, 128), F32),
        in_specs=[pl.BlockSpec(memory_space=pltpu.HBM)] * 2 + [pl.BlockSpec(memory_space=pltpu.SMEM)] * 3,
        out_specs=pl.BlockSpec(memory_space=pltpu.VMEM),
        scratch_shapes=[
            vmem((2, 12, 128, 128), F32),
            vmem((12, 128, 128), jnp.int32),
            *([slabs] * 9),
            vmem((4, 128, 128), F32),
            vmem((128, 128), F32),
            tile(2),
            tile(3, 2),
            tile(17, 3),
            tile(17, 9),
            tile(17),
            tile(17),
            tile(10),
            tile(16),
            tile(4, 15),
            tile(15),
            tile(15),
            dma((2,)),
            dma((2,)),
            dma((2,)),
            dma((2, 4, 2)),
            dma((2, 4, 2)),
            dma((7,)),
            dma(()),
            dma((16,)),
            dma((16,)),
            dma((7,)),
            dma((8,)),
            dma((16,)),
            dma((16,)),
            dma((6,)),
            dma((6,)),
            dma((16,)),
            dma((16,)),
            dma((5,)),
            dma((5,)),
            dma((4,)),
            dma(()),
            pltpu.SemaphoreType.REGULAR((4,)),
        ],
        compiler_params=pltpu.CompilerParams(
            collective_id=0, has_side_effects=True, vmem_limit_bytes=40 * 2**20
        ),
        cost_estimate=pl.CostEstimate(flops=50_000_000, bytes_accessed=2_000_000, transcendentals=500_000),
    )(held(starts[0]), held(materials), conductivity, pre_factor, activation)
    return result[None]


def solution(mesh):
    return jax.shard_map(
        on_device,
        mesh=mesh,
        in_specs=(P("tm", "gz", None, None), P("gz", None, None), P(), P(), P()),
        out_specs=P("tm", "gz", None, None),
        check_vma=False,
    )
```

```python
import functools

import jax
import jax.numpy as jnp
from jax import lax
from jax.experimental import pallas as pl
from jax.experimental.pallas import tpu as pltpu
from jax.sharding import PartitionSpec as P

FSTEPS = 4
CSTEPS = 1
STEP = 0.06
MESH = pl.DeviceIdType.MESH
F32 = jnp.float32
NG = 32
NT = 16


def iota(shape, dim):
    return lax.broadcasted_iota(jnp.int32, shape, dim)


def ones_where(mask):
    return jnp.where(mask, F32(1.0), F32(0.0))


def lane_dot(x, weights):
    high = x.astype(jnp.bfloat16)
    left = x - high.astype(F32)
    middle = left.astype(jnp.bfloat16)
    low = (left - middle.astype(F32)).astype(jnp.bfloat16)
    weights = weights.astype(jnp.bfloat16)
    return jnp.dot(
        jnp.concatenate([high, middle, low], axis=1),
        jnp.concatenate([weights] * 3, axis=0),
        preferred_element_type=F32,
    )


def pool(totals, rows):
    cols = ones_where(iota((128, 128), 0) // 4 == iota((128, 128), 1) % 32)
    parts = []
    for i, total in enumerate(totals):
        rows[i] = total
        four = [rows[i, pl.ds(q, 32, stride=4)] for q in range(4)]
        parts.append((four[0] + four[1]) + (four[2] + four[3]))
    tall = lane_dot(jnp.concatenate(parts, axis=0), cols)
    group = iota((8, 128), 1) // 32
    outs = []
    for i in range(len(totals)):
        out = jnp.zeros((8, 128), F32)
        for g in range(4):
            at = 32 * i + 8 * g
            out = out + jnp.where(group == g, tall[at : at + 8], F32(0.0))
        outs.append(out * F32(1.0 / 64.0))
    return outs


def unpool(coarse, rows):
    group = iota((8, 128), 1) // 32
    u = jnp.concatenate([jnp.where(group == g, coarse, F32(0.0)) for g in range(4)], axis=0)
    wide = lane_dot(u, ones_where(iota((128, 128), 0) % 32 == iota((128, 128), 1) // 4))
    for q in range(4):
        rows[pl.ds(q, 32, stride=4)] = wide


def release(v, hp, act):
    return hp * jnp.exp(act * v / (1.0 + jnp.abs(v)))


def lookup(ids, table):
    return jnp.where(ids == 0, table[0], jnp.where(ids == 1, table[1], table[2]))


def coarse_shifts(v):
    row = iota(v.shape, 1)
    right = pltpu.roll(v, 127, 2)
    left = pltpu.roll(v, 1, 2)
    up = pltpu.roll(v, 7, 1)
    up = jnp.where(row == 7, pltpu.roll(up, 96, 2), up)
    down = pltpu.roll(v, 1, 1)
    down = jnp.where(row == 0, pltpu.roll(down, 32, 2), down)
    return right, left, up, down


def coarse_coefs(k, p, outside, inside):
    scale = F32(STEP * FSTEPS / CSTEPS / 16.0 * 0.5)
    n = k.shape[0] - 2
    mid = k[1:-1]
    lane = iota(mid.shape, 2)
    row = iota(mid.shape, 1)
    right, left, up, down = coarse_shifts(mid)
    edges = (
        (right, lane % 32 == 31),
        (left, lane % 32 == 0),
        (up, (row == 7) & (lane >= 96)),
        (down, (row == 0) & (lane < 32)),
    )
    keep = F32(1.0)
    sides = []
    for other, edge in edges:
        face = scale * (mid + jnp.where(edge, outside, other))
        keep = keep - face
        sides.append(jnp.where(edge, F32(0.0), face))
    faces = scale * (k[1:] + k[:-1])
    keep = keep - faces[1:] - faces[:-1]
    both = [jnp.where(inside[i] & inside[i + 1], faces[i : i + 1], F32(0.0)) for i in range(n + 1)]
    vertical = jnp.concatenate(both, axis=0)
    return sides, vertical, keep, F32(STEP * FSTEPS / CSTEPS) * p


def coarse_step(c, sides, below, above, keep, hp, act):
    mid = c[1:-1]
    out = mid * keep + below * c[:-2] + above * c[2:]
    for other, face in zip(coarse_shifts(mid), sides):
        out = out + face * other
    return out + release(mid, hp, act)


def kernel(
    starts,
    materials,
    cond_in,
    pre_in,
    act_in,
    out,
    cond,
    pre,
    act,
    rows4,
    fab,
    ids,
    kbuf,
    kz,
    kxr,
    kxl,
    kyu,
    kyd,
    keep,
    hp,
    actb,
    fprev,
    relay,
    oldv,
    near,
    gbuf,
    dbuf,
    c8,
    state,
    gs,
    cz,
    cside,
    ckeep,
    chp,
    local_sem,
    near_s,
    near_r,
    slab_s,
    slab_r,
    c0_s,
    c0_r,
    gc_s,
    gc_r,
    dt_s,
    dt_r,
    dg_s,
    dg_r,
    dl_s,
    dl_r,
    cr_s,
    cr_r,
    f_s,
    f_r,
    st_r,
    rl_s,
    rl_r,
    know,
):
    tm = lax.axis_index("tm")
    gz = lax.axis_index("gz")
    zi = lax.rem(tm, 8)
    hi = tm // 8
    yy = hi * 4 + gz // 8
    rest = lax.rem(gz, 8)

    def ring(k):
        return (hi * 8 + lax.rem(zi + (k % 8), 8), gz)

    def ygo(k):
        y = lax.rem(yy + (k % 8), 8)
        return ((y // 4) * 8 + zi, lax.rem(y, 4) * 8 + rest)

    def has(j):
        return (gz + j >= 0) & (gz + j < NG)

    def has_slice(k):
        return (zi + k >= 0) & (zi + k < 8)

    def remote(src, dst, send, recv, where):
        return pltpu.make_async_remote_copy(
            src_ref=src, dst_ref=dst, send_sem=send, recv_sem=recv, device_id=where, device_id_type=MESH
        )

    pending = []

    def send(when, *copies):
        @pl.when(when)
        def _():
            for copy in copies:
                copy().start()

        pending.append((when, copies))

    def finish():
        for when, copies in pending:

            @pl.when(when)
            def _(copies=copies):
                for copy in copies:
                    copy().wait_send()

    def tell_one(sem, where):
        pl.semaphore_signal(sem, 1, device_id=where, device_id_type=MESH)

    def tell(sem, dist):
        for j in (-dist, dist):

            @pl.when(has(j))
            def _():
                tell_one(sem, (tm, gz + j))

            @pl.when(has_slice(j))
            def _():
                tell_one(sem, (tm + j, gz))

        tell_one(sem, ygo(dist))
        if dist < 4:
            tell_one(sem, ygo(-dist))

    def hear(sem, dist):
        n = 1 if dist == 4 else 2
        for j in (-dist, dist):
            n = n + has(j).astype(jnp.int32) + has_slice(j).astype(jnp.int32)
        pl.semaphore_wait(sem, n)

    is_b = hi == 1
    is_a = jnp.logical_not(is_b)

    own_f = pltpu.make_async_copy(starts, fab.at[0, pl.ds(4, 4)], local_sem.at[0])
    own_m = pltpu.make_async_copy(materials, ids.at[pl.ds(4, 4)], local_sem.at[1])
    tables = [
        pltpu.make_async_copy(src, dst, local_sem.at[2 + i])
        for i, (src, dst) in enumerate(((cond_in, cond), (pre_in, pre), (act_in, act)))
    ]
    for table in tables:
        table.start()
    own_m.start()
    own_f.start()
    for j, at in ((-1, 0), (1, 8)):

        @pl.when(jnp.logical_not(has(j)))
        def _():
            fab[0, pl.ds(at, 4)] = jnp.zeros((4, 128, 128), F32)
            ids[pl.ds(at, 4)] = jnp.zeros((4, 128, 128), jnp.int32)

    near[...] = jnp.zeros(near.shape, F32)
    gbuf[...] = jnp.zeros(gbuf.shape, F32)
    dbuf[...] = jnp.zeros(dbuf.shape, F32)
    c8[...] = jnp.zeros(c8.shape, F32)

    barrier = pltpu.get_barrier_semaphore()
    tell(barrier, 1)

    for table in tables:
        table.wait()
    c0 = cond[0]
    own_m.wait()
    totals = [jnp.zeros((128, 128), F32) for _ in range(3)]
    for n in range(4):
        layer = ids[4 + n]
        totals = [t + lookup(layer, table) for t, table in zip(totals, (cond, pre, act))]
    own_f.wait()
    totals.append(fab[0, 4] + fab[0, 5] + fab[0, 6] + fab[0, 7])
    pooled = pool(totals, rows4)
    for i in range(3):
        gbuf[8, i] = pooled[i]
    own_coarse = pooled[3]
    near[1, 0] = pooled[0]
    near[1, 1] = own_coarse

    @pl.when(tm == 0)
    def _():
        dbuf[8, 0] = own_coarse
        out[...] = fab[0, pl.ds(4, 4)]

    hear(barrier, 1)

    def near_copy(j):
        side = 0 if j > 0 else 1
        return remote(near.at[1], near.at[1 - j], near_s.at[side], near_r.at[side], (tm, gz + j))

    def slab(j, n, what):
        side = 0 if j > 0 else 1
        here = 3 - n if j > 0 else n
        there = here if j > 0 else 8 + here
        src = (starts if what == 0 else materials).at[here]
        dst = fab.at[0, there] if what == 0 else ids.at[there]
        return remote(src, dst, slab_s.at[side, n, what], slab_r.at[side, n, what], (tm, gz + j))

    for j in (1, -1):
        send(has(j), functools.partial(near_copy, j))
    for n in range(4):
        for j in (1, -1):
            send(has(j), functools.partial(slab, j, n, 1), functools.partial(slab, j, n, 0))
    tell(know.at[0], 1)

    lane = iota((128, 128), 1)
    row = iota((128, 128), 0)
    half = F32(0.5 * STEP)

    def inside_fine(layer):
        return jnp.logical_not(((layer < 4) & (gz == 0)) | ((layer >= 8) & (gz == NG - 1)))

    def sources(layer):
        ident, inside = ids[layer], inside_fine(layer)
        kbuf[layer] = lookup(ident, cond)
        hp[layer] = jnp.where(inside, F32(STEP) * lookup(ident, pre), F32(0.0))
        actb[layer] = lookup(ident, act)

    def faces(layer):
        k = kbuf[layer]
        inside = inside_fine(layer)
        above = half * (k + kbuf[layer + 1])
        below = half * (k + kbuf[layer - 1])
        rest_of = 1.0 - above - below
        for other, edge, ref in (
            (pltpu.roll(k, 127, 1), lane == 127, kxr),
            (pltpu.roll(k, 1, 1), lane == 0, kxl),
            (pltpu.roll(k, 127, 0), row == 127, kyu),
            (pltpu.roll(k, 1, 0), row == 0, kyd),
        ):
            face = half * (k + jnp.where(edge, c0, other))
            rest_of = rest_of - face
            ref[layer] = jnp.where(edge, F32(0.0), face)
        keep[layer] = rest_of
        kz[layer] = jnp.where(inside & inside_fine(layer + 1), above, F32(0.0))
        kz[layer - 1] = jnp.where(inside & inside_fine(layer - 1), below, F32(0.0))

    def fine_step(layer, at):
        v = fab[at, layer]
        new = v * keep[layer] + kz[layer - 1] * fab[at, layer - 1] + kz[layer] * fab[at, layer + 1]
        new = new + kxr[layer] * pltpu.roll(v, 127, 1) + kxl[layer] * pltpu.roll(v, 1, 1)
        new = new + kyu[layer] * pltpu.roll(v, 127, 0) + kyd[layer] * pltpu.roll(v, 1, 0)
        fab[1 - at, layer] = new + release(v, hp[layer], actb[layer])

    def slab_here(n, what):
        for j in (1, -1):

            @pl.when(has(-j))
            def _():
                slab(j, n, what).wait_recv()

    def stage(n):
        if n > 0:
            fine_step(5, n % 2)
            fine_step(6, n % 2)
        slab_here(n, 1)
        sources(3 - n)
        sources(8 + n)
        if n == 0:

            def own_faces(i, _):
                faces(4 + i)
                return 0

            lax.fori_loop(0, 4, own_faces, 0)
        else:
            faces(4 - n)
            faces(7 + n)
        slab_here(n, 0)

        def pair(i, _):
            at = lax.rem(i, 2)
            fine_step(4 - n + i, at)
            fine_step(7 + n - i, at)
            return 0

        lax.fori_loop(0, n + 1, pair, 0)
        if n == 0:
            fine_step(5, 0)
            fine_step(6, 0)

    def own_sources(i, _):
        sources(4 + i)
        return 0

    lax.fori_loop(0, 4, own_sources, 0)
    hear(know.at[0], 1)
    tell(know.at[1], 2)
    for j in (1, -1):

        @pl.when(has(-j))
        def _():
            near_copy(j).wait_recv()

    @pl.when(jnp.logical_not(has(-1)))
    def _():
        near[0, 0] = jnp.full((8, 128), c0, F32)

    @pl.when(jnp.logical_not(has(1)))
    def _():
        near[2, 0] = jnp.full((8, 128), c0, F32)

    sides, vertical, kept, heat = coarse_coefs(
        near[:, 0], gbuf[8, 1][None], c0, [has(-1), has(0), has(1)]
    )
    old = coarse_step(near[:, 1], sides, vertical[:1], vertical[1:], kept, heat, gbuf[8, 2][None])[0]
    oldv[0] = old

    hear(know.at[1], 2)
    tell(know.at[2], 4)
    for n in range(3):
        stage(n)

    def gc_copy(j):
        i = j + 8 if j < 0 else j + 7
        return remote(gbuf.at[8], gbuf.at[8 - j], gc_s.at[i], gc_r.at[i], (tm, gz + j))

    def c0_copy(n):
        return remote(dbuf.at[8, 0], dbuf.at[8, 0], c0_s.at[n - 1], c0_r, (n, gz))

    around = [j for d in range(1, 9) for j in (d, -d)]

    def coarse_out(when):
        @pl.when(when)
        def _():
            hear(know.at[2], 4)
            tell_one(know.at[3], ygo(4))
            tell_one(know.at[3], ring(1))
            tell_one(know.at[3], ring(-1))

        for j in around:
            send(when & has(j), functools.partial(gc_copy, j))

    late = zi >= 4
    coarse_out(late)
    stage(3)

    def pass_old():
        return remote(oldv.at[0], oldv.at[1], f_s.at[4], f_r.at[4], (tm + 1, gz))

    def pass_fine(n):
        return remote(fab.at[0, 4 + n], fprev.at[n], f_s.at[n], f_r.at[n], (tm + 1, gz))

    def pass_strip(n):
        strip = pl.ds(0, 32)
        return remote(fab.at[0, 4 + n, strip], fprev.at[n, strip], f_s.at[n], st_r.at[n - 1], (8, gz))

    def to_relay(n):
        return remote(fab.at[0, 4 + n, pl.ds(32, 96)], relay, rl_s.at[n], rl_r, (n + 3, gz))

    def from_relay(n):
        return remote(relay, fprev.at[n, pl.ds(32, 96)], rl_s.at[0], f_r.at[n], (8, gz))

    send(tm == 7, *[functools.partial(to_relay, n) for n in range(1, 4)])

    @pl.when(tm == 7)
    def _():
        pl.semaphore_wait(know.at[3], 3)

    send(
        tm == 7, functools.partial(pass_fine, 0), *[functools.partial(pass_strip, n) for n in range(1, 4)], pass_old
    )
    dbuf[8, zi + 1] = pool([fab[0, 4] + fab[0, 5] + fab[0, 6] + fab[0, 7]], rows4)[0] - old
    coarse_out(jnp.logical_not(late))

    send(tm == 0, *[functools.partial(c0_copy, n) for n in range(1, 8)])

    def dt_copy(k):
        own = dbuf.at[8, zi + 1]
        return remote(own, own, dt_s.at[k - 1], dt_r.at[zi], ring(k))

    send(tm >= 0, *[functools.partial(dt_copy, k) for k in (4, 3, 5, 2, 6, 1, 7)])

    def dt_here(first, last):
        for at in range(first, last):

            @pl.when(zi != at)
            def _():
                that = dbuf.at[8, at + 1]
                remote(that, that, dt_s.at[0], dt_r.at[at], ring(1)).wait_recv()

    whole = [pass_old] + [functools.partial(pass_fine, n) for n in range(4)]
    send(zi < 2, *whole)

    def dg_copy(j):
        i = j + 8 if j < 0 else j + 7
        some = pl.ds(0, min(5, 9 - abs(j)))
        return remote(dbuf.at[8, some], dbuf.at[8 - j, some], dg_s.at[i], dg_r.at[i], (tm, gz + j))

    def dl_copy(j):
        i = j + 3 if j < 0 else j + 2
        some = pl.ds(5, 4 - abs(j))
        return remote(dbuf.at[8, some], dbuf.at[8 - j, some], dl_s.at[i], dl_r.at[i], (tm, gz + j))

    @pl.when((tm > 0) & (tm < 8))
    def _():
        c0_copy(1).wait_recv()

    dt_here(0, 4)
    for j in around[::-1]:
        send(has(j), functools.partial(dg_copy, j))
    for n in range(1, 4):

        @pl.when(tm == n + 3)
        def _():
            to_relay(n).wait_recv()

        send(tm == n + 3, functools.partial(from_relay, n))
    dt_here(4, 7)
    for j in around[:6][::-1]:
        send(has(j), functools.partial(dl_copy, j))
    send((zi >= 2) & (zi < 7), *whole)

    for j in around:

        @pl.when(has(-j))
        def _():
            gc_copy(j).wait_recv()

    k_all = jnp.concatenate(
        [jnp.where(has(j), gbuf[j + 8 : j + 9, 0], c0) for j in range(-8, 9)], axis=0
    )
    sides, vertical, kept, heat = coarse_coefs(k_all, gbuf[1:16, 1], c0, [has(j) for j in range(-8, 9)])
    for i in range(4):
        cside[i] = sides[i]
    cz[...] = vertical
    ckeep[...] = kept
    chp[...] = heat

    def cr_copy(j):
        return remote(gs.at[9], c8.at[8 - j], cr_s.at[j + 7], cr_r.at[j + 7], (tm + 8, gz + j))

    def g8_copy():
        return remote(gs.at[8], gs.at[0], cr_s.at[15], cr_r.at[15], (8, gz))

    for j in around:

        @pl.when(has(-j))
        def _():
            dg_copy(j).wait_recv()

    for j in range(-7, 8):

        @pl.when(is_b & has(-j) & (zi >= abs(j)))
        def _():
            cr_copy(j).wait_recv()

    state[...] = jnp.where(is_b, c8[...], dbuf[:, 0])
    for s in range(1, 9):
        if s == 5:
            for j in around[:6]:

                @pl.when(has(-j))
                def _():
                    dl_copy(j).wait_recv()

        if s == 8:
            dt_here(7, 8)

        @pl.when(is_a | (zi >= s))
        def _():
            n = 17 - 2 * s
            lo = s - 1
            latest = coarse_step(
                state[pl.ds(lo, n + 2)],
                [cside[i, pl.ds(lo, n)] for i in range(4)],
                cz[pl.ds(lo, n)],
                cz[pl.ds(lo + 1, n)],
                ckeep[pl.ds(lo, n)],
                chp[pl.ds(lo, n)],
                gbuf[pl.ds(s, n), 2],
            )
            gs[s] = latest[8 - s]
            state[pl.ds(s, n)] = latest + dbuf[pl.ds(s, n), s]

    @pl.when(is_a)
    def _():
        gs[9] = state[8]

    @pl.when(tm != 7)
    def _():
        pl.semaphore_wait(know.at[3], 3)

    send(tm == 0, g8_copy)
    for j in sorted(range(-7, 8), key=lambda j: -abs(j)):
        send((tm < 8) & (zi >= abs(j)) & has(j), functools.partial(cr_copy, j))

    @pl.when(tm == 8)
    def _():
        g8_copy().wait_recv()

    @pl.when(tm > 0)
    def _():
        pass_old().wait_recv()
        unpool(gs[zi] - oldv[1], rows4.at[0])

        @pl.when(tm != 8)
        def _():
            for n in range(4):
                pass_fine(n).wait_recv()

        @pl.when(tm == 8)
        def _():
            pass_fine(0).wait_recv()
            for n in range(1, 4):
                pass_strip(n).wait_recv()
                from_relay(n).wait_recv()

        fine = rows4[0]
        for n in range(4):
            out[n] = fprev[n] + fine

    finish()


def on_device(starts, materials, conductivity, pre_factor, activation):
    vmem, dma = pltpu.VMEM, pltpu.SemaphoreType.DMA
    slabs = vmem((12, 128, 128), F32)
    tile = lambda *lead: vmem(lead + (8, 128), F32)
    held = lambda x: pltpu.with_memory_space_constraint(x, pltpu.HBM)
    result = pl.pallas_call(
        kernel,
        name="parareal",
        out_shape=jax.ShapeDtypeStruct((4, 128, 128), F32),
        in_specs=[pl.BlockSpec(memory_space=pltpu.HBM)] * 5,
        out_specs=pl.BlockSpec(memory_space=pltpu.VMEM),
        scratch_shapes=[
            *([pltpu.SMEM((3,), F32)] * 3),
            vmem((4, 128, 128), F32),
            vmem((2, 12, 128, 128), F32),
            vmem((12, 128, 128), jnp.int32),
            *([slabs] * 9),
            vmem((4, 128, 128), F32),
            vmem((96, 128), F32),
            tile(2),
            tile(3, 2),
            tile(17, 3),
            tile(17, 9),
            tile(17),
            tile(17),
            tile(10),
            tile(16),
            tile(4, 15),
            tile(15),
            tile(15),
            dma((5,)),
            dma((2,)),
            dma((2,)),
            dma((2, 4, 2)),
            dma((2, 4, 2)),
            dma((7,)),
            dma(()),
            dma((16,)),
            dma((16,)),
            dma((7,)),
            dma((8,)),
            dma((16,)),
            dma((16,)),
            dma((6,)),
            dma((6,)),
            dma((16,)),
            dma((16,)),
            dma((5,)),
            dma((5,)),
            dma((3,)),
            dma((4,)),
            dma(()),
            pltpu.SemaphoreType.REGULAR((4,)),
        ],
        compiler_params=pltpu.CompilerParams(
            collective_id=0, has_side_effects=True, vmem_limit_bytes=40 * 2**20
        ),
        cost_estimate=pl.CostEstimate(flops=50_000_000, bytes_accessed=2_000_000, transcendentals=500_000),
    )(held(starts[0]), held(materials), held(conductivity), held(pre_factor), held(activation))
    return result[None]


def solution(mesh):
    return jax.shard_map(
        on_device,
        mesh=mesh,
        in_specs=(P("tm", "gz", None, None), P("gz", None, None), P(), P(), P()),
        out_specs=P("tm", "gz", None, None),
        check_vma=False,
    )
```

```python
import functools

import jax
import jax.numpy as jnp
from jax import lax
from jax.experimental import pallas as pl
from jax.experimental.pallas import tpu as pltpu
from jax.sharding import PartitionSpec as P

FSTEPS = 4
CSTEPS = 1
STEP = 0.06
MESH = pl.DeviceIdType.MESH
F32 = jnp.float32
NG = 32
NT = 16


def iota(shape, dim):
    return lax.broadcasted_iota(jnp.int32, shape, dim)


def ones_where(mask):
    return jnp.where(mask, F32(1.0), F32(0.0))


def lane_dot(x, weights):
    high = x.astype(jnp.bfloat16)
    left = x - high.astype(F32)
    middle = left.astype(jnp.bfloat16)
    low = (left - middle.astype(F32)).astype(jnp.bfloat16)
    weights = weights.astype(jnp.bfloat16)
    return jnp.dot(
        jnp.concatenate([high, middle, low], axis=1),
        jnp.concatenate([weights] * 3, axis=0),
        preferred_element_type=F32,
    )


def pool(totals, rows):
    cols = ones_where(iota((128, 128), 0) // 4 == iota((128, 128), 1) % 32)
    parts = []
    for i, total in enumerate(totals):
        rows[i] = total
        four = [rows[i, pl.ds(q, 32, stride=4)] for q in range(4)]
        parts.append((four[0] + four[1]) + (four[2] + four[3]))
    tall = lane_dot(jnp.concatenate(parts, axis=0), cols)
    group = iota((8, 128), 1) // 32
    outs = []
    for i in range(len(totals)):
        out = jnp.zeros((8, 128), F32)
        for g in range(4):
            at = 32 * i + 8 * g
            out = out + jnp.where(group == g, tall[at : at + 8], F32(0.0))
        outs.append(out * F32(1.0 / 64.0))
    return outs


def unpool(coarse, rows):
    group = iota((8, 128), 1) // 32
    u = jnp.concatenate([jnp.where(group == g, coarse, F32(0.0)) for g in range(4)], axis=0)
    wide = lane_dot(u, ones_where(iota((128, 128), 0) % 32 == iota((128, 128), 1) // 4))
    for q in range(4):
        rows[pl.ds(q, 32, stride=4)] = wide


def release(v, hp, act):
    return hp * jnp.exp(act * v / (1.0 + jnp.abs(v)))


def lookup(ids, table):
    return jnp.where(ids == 0, table[0], jnp.where(ids == 1, table[1], table[2]))


def coarse_shifts(v):
    row = iota(v.shape, 1)
    right = pltpu.roll(v, 127, 2)
    left = pltpu.roll(v, 1, 2)
    up = pltpu.roll(v, 7, 1)
    up = jnp.where(row == 7, pltpu.roll(up, 96, 2), up)
    down = pltpu.roll(v, 1, 1)
    down = jnp.where(row == 0, pltpu.roll(down, 32, 2), down)
    return right, left, up, down


def coarse_coefs(k, p, outside, inside):
    scale = F32(STEP * FSTEPS / CSTEPS / 16.0 * 0.5)
    n = k.shape[0] - 2
    mid = k[1:-1]
    lane = iota(mid.shape, 2)
    row = iota(mid.shape, 1)
    right, left, up, down = coarse_shifts(mid)
    edges = (
        (right, lane % 32 == 31),
        (left, lane % 32 == 0),
        (up, (row == 7) & (lane >= 96)),
        (down, (row == 0) & (lane < 32)),
    )
    keep = F32(1.0)
    sides = []
    for other, edge in edges:
        face = scale * (mid + jnp.where(edge, outside, other))
        keep = keep - face
        sides.append(jnp.where(edge, F32(0.0), face))
    faces = scale * (k[1:] + k[:-1])
    keep = keep - faces[1:] - faces[:-1]
    both = [jnp.where(inside[i] & inside[i + 1], faces[i : i + 1], F32(0.0)) for i in range(n + 1)]
    vertical = jnp.concatenate(both, axis=0)
    return sides, vertical, keep, F32(STEP * FSTEPS / CSTEPS) * p


def coarse_step(c, sides, below, above, keep, hp, act):
    mid = c[1:-1]
    out = mid * keep + below * c[:-2] + above * c[2:]
    for other, face in zip(coarse_shifts(mid), sides):
        out = out + face * other
    return out + release(mid, hp, act)


def kernel(
    starts,
    materials,
    cond_in,
    pre_in,
    act_in,
    out,
    cond,
    pre,
    act,
    rows4,
    fab,
    ids,
    kbuf,
    kz,
    kxr,
    kxl,
    kyu,
    kyd,
    keep,
    hp,
    actb,
    fprev,
    relay,
    ownd,
    oldv,
    near,
    gbuf,
    dbuf,
    c8,
    state,
    gs,
    cz,
    cside,
    ckeep,
    chp,
    local_sem,
    near_s,
    near_r,
    slab_s,
    slab_r,
    c0_s,
    c0_r,
    gc_s,
    gc_r,
    dt_s,
    dt_r,
    dg_s,
    dg_r,
    dl_s,
    dl_r,
    cr_s,
    cr_r,
    f_s,
    f_r,
    part_r,
    rl_s,
    rl_r,
    know,
):
    tm = lax.axis_index("tm")
    gz = lax.axis_index("gz")
    zi = lax.rem(tm, 8)
    hi = tm // 8
    yy = hi * 4 + gz // 8
    rest = lax.rem(gz, 8)

    def ring(k):
        return (hi * 8 + lax.rem(zi + (k % 8), 8), gz)

    def ygo(k):
        y = lax.rem(yy + (k % 8), 8)
        return ((y // 4) * 8 + zi, lax.rem(y, 4) * 8 + rest)

    def has(j):
        return (gz + j >= 0) & (gz + j < NG)

    def has_slice(k):
        return (zi + k >= 0) & (zi + k < 8)

    def remote(src, dst, send, recv, where):
        return pltpu.make_async_remote_copy(
            src_ref=src, dst_ref=dst, send_sem=send, recv_sem=recv, device_id=where, device_id_type=MESH
        )

    pending = []

    def send(when, *copies):
        @pl.when(when)
        def _():
            for copy in copies:
                copy().start()

        pending.append((when, copies))

    def finish():
        for when, copies in pending:

            @pl.when(when)
            def _(copies=copies):
                for copy in copies:
                    copy().wait_send()

    def tell_one(sem, where):
        pl.semaphore_signal(sem, 1, device_id=where, device_id_type=MESH)

    def tell(sem, dist):
        for j in (-dist, dist):

            @pl.when(has(j))
            def _():
                tell_one(sem, (tm, gz + j))

            @pl.when(has_slice(j))
            def _():
                tell_one(sem, (tm + j, gz))

        tell_one(sem, ygo(dist))
        if dist < 4:
            tell_one(sem, ygo(-dist))

    def hear(sem, dist):
        n = 1 if dist == 4 else 2
        for j in (-dist, dist):
            n = n + has(j).astype(jnp.int32) + has_slice(j).astype(jnp.int32)
        pl.semaphore_wait(sem, n)

    is_b = hi == 1
    is_a = jnp.logical_not(is_b)

    barrier = pltpu.get_barrier_semaphore()
    tell(barrier, 1)
    own_f = pltpu.make_async_copy(starts, fab.at[0, pl.ds(4, 4)], local_sem.at[0])
    own_m = pltpu.make_async_copy(materials, ids.at[pl.ds(4, 4)], local_sem.at[1])
    tables = [
        pltpu.make_async_copy(src, dst, local_sem.at[2 + i])
        for i, (src, dst) in enumerate(((cond_in, cond), (pre_in, pre), (act_in, act)))
    ]
    for table in tables:
        table.start()
    own_m.start()
    own_f.start()

    for j, at in ((-1, 0), (1, 8)):

        @pl.when(jnp.logical_not(has(j)))
        def _():
            fab[0, pl.ds(at, 4)] = jnp.zeros((4, 128, 128), F32)
            ids[pl.ds(at, 4)] = jnp.zeros((4, 128, 128), jnp.int32)
            near[1 + j] = jnp.zeros((2, 8, 128), F32)

    for j in range(-8, 9):

        @pl.when(jnp.logical_not(has(j)))
        def _():
            gbuf[8 + j] = jnp.zeros((3, 8, 128), F32)
            dbuf[8 + j] = jnp.zeros((9, 8, 128), F32)
            c8[8 + j] = jnp.zeros((8, 128), F32)

    for table in tables:
        table.wait()
    c0 = cond[0]
    own_m.wait()
    totals = [jnp.zeros((128, 128), F32) for _ in range(3)]
    for n in range(4):
        layer = ids[4 + n]
        totals = [t + lookup(layer, table) for t, table in zip(totals, (cond, pre, act))]
    own_f.wait()
    totals.append(fab[0, 4] + fab[0, 5] + fab[0, 6] + fab[0, 7])
    pooled = pool(totals, rows4)
    for i in range(3):
        gbuf[8, i] = pooled[i]
    own_coarse = pooled[3]
    near[1, 0] = pooled[0]
    near[1, 1] = own_coarse

    @pl.when(tm == 0)
    def _():
        dbuf[8, 0] = own_coarse
        out[...] = fab[0, pl.ds(4, 4)]

    hear(barrier, 1)

    def near_copy(j):
        side = 0 if j > 0 else 1
        return remote(near.at[1], near.at[1 - j], near_s.at[side], near_r.at[side], (tm, gz + j))

    def slab(j, n, what):
        side = 0 if j > 0 else 1
        here = 3 - n if j > 0 else n
        there = here if j > 0 else 8 + here
        src = (starts if what == 0 else materials).at[here]
        dst = fab.at[0, there] if what == 0 else ids.at[there]
        return remote(src, dst, slab_s.at[side, n, what], slab_r.at[side, n, what], (tm, gz + j))

    for j in (1, -1):
        send(has(j), functools.partial(near_copy, j))
    for n in range(4):
        for j in (1, -1):
            send(has(j), functools.partial(slab, j, n, 1), functools.partial(slab, j, n, 0))
    tell(know.at[0], 1)

    lane = iota((128, 128), 1)
    row = iota((128, 128), 0)
    half = F32(0.5 * STEP)

    def inside_fine(layer):
        return jnp.logical_not(((layer < 4) & (gz == 0)) | ((layer >= 8) & (gz == NG - 1)))

    def sources(layer):
        ident, inside = ids[layer], inside_fine(layer)
        kbuf[layer] = lookup(ident, cond)
        hp[layer] = jnp.where(inside, F32(STEP) * lookup(ident, pre), F32(0.0))
        actb[layer] = lookup(ident, act)

    def faces(layer):
        k = kbuf[layer]
        inside = inside_fine(layer)
        above = half * (k + kbuf[layer + 1])
        below = half * (k + kbuf[layer - 1])
        rest_of = 1.0 - above - below
        for other, edge, ref in (
            (pltpu.roll(k, 127, 1), lane == 127, kxr),
            (pltpu.roll(k, 1, 1), lane == 0, kxl),
            (pltpu.roll(k, 127, 0), row == 127, kyu),
            (pltpu.roll(k, 1, 0), row == 0, kyd),
        ):
            face = half * (k + jnp.where(edge, c0, other))
            rest_of = rest_of - face
            ref[layer] = jnp.where(edge, F32(0.0), face)
        keep[layer] = rest_of
        kz[layer] = jnp.where(inside & inside_fine(layer + 1), above, F32(0.0))
        kz[layer - 1] = jnp.where(inside & inside_fine(layer - 1), below, F32(0.0))

    def fine_step(layer, at):
        v = fab[at, layer]
        new = v * keep[layer] + kz[layer - 1] * fab[at, layer - 1] + kz[layer] * fab[at, layer + 1]
        new = new + kxr[layer] * pltpu.roll(v, 127, 1) + kxl[layer] * pltpu.roll(v, 1, 1)
        new = new + kyu[layer] * pltpu.roll(v, 127, 0) + kyd[layer] * pltpu.roll(v, 1, 0)
        fab[1 - at, layer] = new + release(v, hp[layer], actb[layer])

    def slab_here(n, what):
        for j in (1, -1):

            @pl.when(has(-j))
            def _():
                slab(j, n, what).wait_recv()

    def stage(n):
        if n > 0:
            fine_step(5, n % 2)
            fine_step(6, n % 2)
        slab_here(n, 1)
        sources(3 - n)
        sources(8 + n)
        if n == 0:

            def own_faces(i, _):
                faces(4 + i)
                return 0

            lax.fori_loop(0, 4, own_faces, 0)
        else:
            faces(4 - n)
            faces(7 + n)
        slab_here(n, 0)

        def pair(i, _):
            at = lax.rem(i, 2)
            fine_step(4 - n + i, at)
            fine_step(7 + n - i, at)
            return 0

        lax.fori_loop(0, n + 1, pair, 0)
        if n == 0:
            fine_step(5, 0)
            fine_step(6, 0)

    def own_sources(i, _):
        sources(4 + i)
        return 0

    lax.fori_loop(0, 4, own_sources, 0)
    hear(know.at[0], 1)
    tell(know.at[1], 2)
    for j in (1, -1):

        @pl.when(has(-j))
        def _():
            near_copy(j).wait_recv()

    @pl.when(jnp.logical_not(has(-1)))
    def _():
        near[0, 0] = jnp.full((8, 128), c0, F32)

    @pl.when(jnp.logical_not(has(1)))
    def _():
        near[2, 0] = jnp.full((8, 128), c0, F32)

    sides, vertical, kept, heat = coarse_coefs(
        near[:, 0], gbuf[8, 1][None], c0, [has(-1), has(0), has(1)]
    )
    old = coarse_step(near[:, 1], sides, vertical[:1], vertical[1:], kept, heat, gbuf[8, 2][None])[0]
    oldv[0] = old

    hear(know.at[1], 2)
    tell(know.at[2], 4)
    for n in range(3):
        stage(n)

    def gc_copy(j):
        i = j + 8 if j < 0 else j + 7
        return remote(gbuf.at[8], gbuf.at[8 - j], gc_s.at[i], gc_r.at[i], (tm, gz + j))

    def c0_copy(n):
        return remote(dbuf.at[8, 0], dbuf.at[8, 0], c0_s.at[n - 1], c0_r, (n, gz))

    around = [j for d in range(1, 9) for j in (d, -d)]

    def coarse_out(when):
        @pl.when(when)
        def _():
            hear(know.at[2], 4)
            tell_one(know.at[3], ygo(4))
            tell_one(know.at[3], ring(1))
            tell_one(know.at[3], ring(-1))

        for j in around:
            send(when & has(j), functools.partial(gc_copy, j))

    late = zi >= 4
    coarse_out(late)
    stage(3)

    def pass_old():
        return remote(oldv.at[0], oldv.at[1], f_s.at[4], f_r.at[4], (tm + 1, gz))

    def pass_fine(n):
        return remote(fab.at[0, 4 + n], fprev.at[n], f_s.at[n], f_r.at[n], (tm + 1, gz))

    straight = ((1, 112, 16), (2, 112, 16), (3, 112, 16))

    def pass_part(i):
        layer, first, count = straight[i]
        part = pl.ds(first, count)
        return remote(fab.at[0, 4 + layer, part], fprev.at[layer, part], f_s.at[1 + i], part_r.at[4 + i], (8, gz))

    ways = ((1, 0, 112), (2, 0, 112), (3, 0, 112))
    by = (0, 6, 5)

    def to_relay(i):
        layer, first, count = ways[i]
        return remote(
            fab.at[0, 4 + layer, pl.ds(first, count)], relay.at[pl.ds(0, count)], rl_s.at[i], rl_r, (by[i], gz)
        )

    def from_relay(i):
        layer, first, count = ways[i]
        return remote(
            relay.at[pl.ds(0, count)], fprev.at[layer, pl.ds(first, count)], rl_s.at[5], part_r.at[i], (8, gz)
        )

    def relay_on(i):
        @pl.when(tm == by[i])
        def _():
            to_relay(i).wait_recv()

        send(tm == by[i], functools.partial(from_relay, i))

    def c0_here(when):
        @pl.when(when)
        def _():
            c0_copy(1).wait_recv()

    send(tm == 7, *[functools.partial(to_relay, i) for i in range(len(ways))])
    c0_here(tm == 7)
    parts = [functools.partial(pass_part, i) for i in range(len(straight))]
    send(tm == 7, functools.partial(pass_fine, 0), *parts, pass_old)
    ownd[0] = pool([fab[0, 4] + fab[0, 5] + fab[0, 6] + fab[0, 7]], rows4)[0] - old

    eight = tm == 8

    @pl.when(jnp.logical_not(eight))
    def _():
        dbuf[8, zi + 1] = ownd[0]

    coarse_out(jnp.logical_not(late))

    send(tm == 0, *[functools.partial(c0_copy, n) for n in range(1, 9)])

    def dt_copy(k):
        return remote(ownd.at[0], dbuf.at[8, zi + 1], dt_s.at[k - 1], dt_r.at[zi], ring(k))

    def d8_copy():
        return remote(ownd.at[0], dbuf.at[8, zi + 1], dt_s.at[7], dt_r.at[zi], (8, gz))

    send(tm < 5, d8_copy)
    for k in (4, 3, 5, 2, 6, 1, 7):
        send(jnp.logical_not(is_b & (lax.rem(zi + k, 8) == 0)), functools.partial(dt_copy, k))

    def dt_here(first, last, when):
        for at in range(first, last):

            @pl.when(when & (jnp.logical_not(eight) & (zi != at) if at == 7 else eight | (zi != at)))
            def _():
                that = dbuf.at[8, at + 1]
                remote(that, that, dt_s.at[0], dt_r.at[at], ring(1)).wait_recv()

    whole = [pass_old] + [functools.partial(pass_fine, n) for n in range(4)]
    send(zi < 2, *whole)

    asks = (tm == 5) | (tm == 6)
    dt_here(0, 1, asks)
    send(asks, d8_copy)

    def dg_copy(j):
        i = j + 8 if j < 0 else j + 7
        some = pl.ds(0, min(5, 9 - abs(j)))
        return remote(dbuf.at[8, some], dbuf.at[8 - j, some], dg_s.at[i], dg_r.at[i], (tm, gz + j))

    def dl_copy(j):
        i = j + 3 if j < 0 else j + 2
        some = pl.ds(5, 4 - abs(j))
        return remote(dbuf.at[8, some], dbuf.at[8 - j, some], dl_s.at[i], dl_r.at[i], (tm, gz + j))

    c0_here((tm > 0) & (tm <= 8) & (tm != 7))

    dt_here(0, 1, jnp.logical_not(asks))
    dt_here(1, 4, tm >= 0)
    for j in around[::-1]:
        send(has(j), functools.partial(dg_copy, j))
    for i in range(len(ways)):
        relay_on(i)
    dt_here(4, 7, tm >= 0)
    for j in around[:6][::-1]:
        send(has(j), functools.partial(dl_copy, j))
    send((zi >= 2) & (zi < 7), *whole)

    for j in around:

        @pl.when(has(-j))
        def _():
            gc_copy(j).wait_recv()

    k_all = jnp.concatenate(
        [jnp.where(has(j), gbuf[j + 8 : j + 9, 0], c0) for j in range(-8, 9)], axis=0
    )
    sides, vertical, kept, heat = coarse_coefs(k_all, gbuf[1:16, 1], c0, [has(j) for j in range(-8, 9)])
    for i in range(4):
        cside[i] = sides[i]
    cz[...] = vertical
    ckeep[...] = kept
    chp[...] = heat

    def cr_copy(j):
        return remote(gs.at[9], c8.at[8 - j], cr_s.at[j + 7], cr_r.at[j + 7], (tm + 8, gz + j))

    for j in around:

        @pl.when(has(-j))
        def _():
            dg_copy(j).wait_recv()

    for j in range(-7, 8):

        @pl.when((tm > 8) & has(-j) & (zi >= abs(j)))
        def _():
            cr_copy(j).wait_recv()

    state[...] = jnp.where(tm > 8, c8[...], dbuf[:, 0])
    for s in range(1, 9):
        if s == 5:
            for j in around[:6]:

                @pl.when(has(-j))
                def _():
                    dl_copy(j).wait_recv()

        if s == 8:
            dt_here(7, 8, tm >= 0)

        @pl.when((tm <= 8) | (zi >= s))
        def _():
            n = 17 - 2 * s
            lo = s - 1
            latest = coarse_step(
                state[pl.ds(lo, n + 2)],
                [cside[i, pl.ds(lo, n)] for i in range(4)],
                cz[pl.ds(lo, n)],
                cz[pl.ds(lo + 1, n)],
                ckeep[pl.ds(lo, n)],
                chp[pl.ds(lo, n)],
                gbuf[pl.ds(s, n), 2],
            )
            gs[s] = latest[8 - s]
            state[pl.ds(s, n)] = latest + dbuf[pl.ds(s, n), s]

    @pl.when(is_a)
    def _():
        gs[9] = state[8]

    pl.semaphore_wait(know.at[3], 3)
    for j in sorted(range(-7, 8), key=lambda j: -abs(j)):
        send((tm > 0) & (tm < 8) & (zi >= abs(j)) & has(j), functools.partial(cr_copy, j))

    @pl.when(tm > 0)
    def _():
        pass_old().wait_recv()
        unpool(gs[jnp.where(eight, 8, zi)] - oldv[1], rows4.at[0])

        @pl.when(tm != 8)
        def _():
            for n in range(4):
                pass_fine(n).wait_recv()

        @pl.when(tm == 8)
        def _():
            pass_fine(0).wait_recv()
            for i in range(len(straight)):
                pass_part(i).wait_recv()
            for i in range(len(ways)):
                from_relay(i).wait_recv()

        fine = rows4[0]
        for n in range(4):
            out[n] = fprev[n] + fine

    finish()


def on_device(starts, materials, conductivity, pre_factor, activation):
    vmem, dma = pltpu.VMEM, pltpu.SemaphoreType.DMA
    slabs = vmem((12, 128, 128), F32)
    tile = lambda *lead: vmem(lead + (8, 128), F32)
    held = lambda x: pltpu.with_memory_space_constraint(x, pltpu.HBM)
    result = pl.pallas_call(
        kernel,
        name="parareal",
        out_shape=jax.ShapeDtypeStruct((4, 128, 128), F32),
        in_specs=[pl.BlockSpec(memory_space=pltpu.HBM)] * 5,
        out_specs=pl.BlockSpec(memory_space=pltpu.VMEM),
        scratch_shapes=[
            *([pltpu.SMEM((3,), F32)] * 3),
            vmem((4, 128, 128), F32),
            vmem((2, 12, 128, 128), F32),
            vmem((12, 128, 128), jnp.int32),
            *([slabs] * 9),
            vmem((4, 128, 128), F32),
            vmem((128, 128), F32),
            tile(1),
            tile(2),
            tile(3, 2),
            tile(17, 3),
            tile(17, 9),
            tile(17),
            tile(17),
            tile(10),
            tile(16),
            tile(4, 15),
            tile(15),
            tile(15),
            dma((5,)),
            dma((2,)),
            dma((2,)),
            dma((2, 4, 2)),
            dma((2, 4, 2)),
            dma((8,)),
            dma(()),
            dma((16,)),
            dma((16,)),
            dma((8,)),
            dma((8,)),
            dma((16,)),
            dma((16,)),
            dma((6,)),
            dma((6,)),
            dma((16,)),
            dma((16,)),
            dma((5,)),
            dma((5,)),
            dma((8,)),
            dma((6,)),
            dma(()),
            pltpu.SemaphoreType.REGULAR((4,)),
        ],
        compiler_params=pltpu.CompilerParams(
            collective_id=0, has_side_effects=True, vmem_limit_bytes=40 * 2**20
        ),
        cost_estimate=pl.CostEstimate(flops=50_000_000, bytes_accessed=2_000_000, transcendentals=500_000),
    )(held(starts[0]), held(materials), held(conductivity), held(pre_factor), held(activation))
    return result[None]


def solution(mesh):
    return jax.shard_map(
        on_device,
        mesh=mesh,
        in_specs=(P("tm", "gz", None, None), P("gz", None, None), P(), P(), P()),
        out_specs=P("tm", "gz", None, None),
        check_vma=False,
    )
```

```python
import functools

import jax
import jax.numpy as jnp
from jax import lax
from jax.experimental import pallas as pl
from jax.experimental.pallas import tpu as pltpu
from jax.sharding import PartitionSpec as P

FSTEPS = 4
CSTEPS = 1
STEP = 0.06
MESH = pl.DeviceIdType.MESH
F32 = jnp.float32
NG = 32
NT = 16


def iota(shape, dim):
    return lax.broadcasted_iota(jnp.int32, shape, dim)


def ones_where(mask):
    return jnp.where(mask, F32(1.0), F32(0.0))


def lane_dot(x, weights):
    high = x.astype(jnp.bfloat16)
    left = x - high.astype(F32)
    middle = left.astype(jnp.bfloat16)
    low = (left - middle.astype(F32)).astype(jnp.bfloat16)
    weights = weights.astype(jnp.bfloat16)
    return jnp.dot(
        jnp.concatenate([high, middle, low], axis=1),
        jnp.concatenate([weights] * 3, axis=0),
        preferred_element_type=F32,
    )


def pool(totals, rows):
    cols = ones_where(iota((128, 128), 0) // 4 == iota((128, 128), 1) % 32)
    parts = []
    for i, total in enumerate(totals):
        rows[i] = total
        four = [rows[i, pl.ds(q, 32, stride=4)] for q in range(4)]
        parts.append((four[0] + four[1]) + (four[2] + four[3]))
    tall = lane_dot(jnp.concatenate(parts, axis=0), cols)
    group = iota((8, 128), 1) // 32
    outs = []
    for i in range(len(totals)):
        out = jnp.zeros((8, 128), F32)
        for g in range(4):
            at = 32 * i + 8 * g
            out = out + jnp.where(group == g, tall[at : at + 8], F32(0.0))
        outs.append(out * F32(1.0 / 64.0))
    return outs


def unpool(coarse, rows):
    group = iota((8, 128), 1) // 32
    u = jnp.concatenate([jnp.where(group == g, coarse, F32(0.0)) for g in range(4)], axis=0)
    wide = lane_dot(u, ones_where(iota((128, 128), 0) % 32 == iota((128, 128), 1) // 4))
    for q in range(4):
        rows[pl.ds(q, 32, stride=4)] = wide


def release(v, hp, act):
    return hp * jnp.exp(act * v / (1.0 + jnp.abs(v)))


def lookup(ids, table):
    return jnp.where(ids == 0, table[0], jnp.where(ids == 1, table[1], table[2]))


def coarse_shifts(v):
    row = iota(v.shape, 1)
    right = pltpu.roll(v, 127, 2)
    left = pltpu.roll(v, 1, 2)
    up = pltpu.roll(v, 7, 1)
    up = jnp.where(row == 7, pltpu.roll(up, 96, 2), up)
    down = pltpu.roll(v, 1, 1)
    down = jnp.where(row == 0, pltpu.roll(down, 32, 2), down)
    return right, left, up, down


def coarse_coefs(k, p, outside, inside):
    scale = F32(STEP * FSTEPS / CSTEPS / 16.0 * 0.5)
    n = k.shape[0] - 2
    mid = k[1:-1]
    lane = iota(mid.shape, 2)
    row = iota(mid.shape, 1)
    right, left, up, down = coarse_shifts(mid)
    edges = (
        (right, lane % 32 == 31),
        (left, lane % 32 == 0),
        (up, (row == 7) & (lane >= 96)),
        (down, (row == 0) & (lane < 32)),
    )
    keep = F32(1.0)
    sides = []
    for other, edge in edges:
        face = scale * (mid + jnp.where(edge, outside, other))
        keep = keep - face
        sides.append(jnp.where(edge, F32(0.0), face))
    faces = scale * (k[1:] + k[:-1])
    keep = keep - faces[1:] - faces[:-1]
    both = [jnp.where(inside[i] & inside[i + 1], faces[i : i + 1], F32(0.0)) for i in range(n + 1)]
    vertical = jnp.concatenate(both, axis=0)
    return sides, vertical, keep, F32(STEP * FSTEPS / CSTEPS) * p


def coarse_step(c, sides, below, above, keep, hp, act):
    mid = c[1:-1]
    out = mid * keep + below * c[:-2] + above * c[2:]
    for other, face in zip(coarse_shifts(mid), sides):
        out = out + face * other
    return out + release(mid, hp, act)


def kernel(
    starts,
    materials,
    cond_in,
    pre_in,
    act_in,
    out,
    cond,
    pre,
    act,
    rows4,
    fab,
    ids,
    kbuf,
    kz,
    kxr,
    kxl,
    kyu,
    kyd,
    keep,
    hp,
    actb,
    fprev,
    relay,
    ownd,
    oldv,
    near,
    gbuf,
    dbuf,
    c8,
    state,
    gs,
    cz,
    cside,
    ckeep,
    chp,
    local_sem,
    near_s,
    near_r,
    slab_s,
    slab_r,
    c0_s,
    c0_r,
    gc_s,
    gc_r,
    dt_s,
    dt_r,
    dg_s,
    dg_r,
    dm_s,
    dm_r,
    dl_s,
    dl_r,
    cr_s,
    cr_r,
    f_s,
    f_r,
    part_r,
    rl_s,
    rl_r,
    know,
):
    tm = lax.axis_index("tm")
    gz = lax.axis_index("gz")
    zi = lax.rem(tm, 8)
    hi = tm // 8
    yy = hi * 4 + gz // 8
    rest = lax.rem(gz, 8)

    def ring(k):
        return (hi * 8 + lax.rem(zi + (k % 8), 8), gz)

    def ygo(k):
        y = lax.rem(yy + (k % 8), 8)
        return ((y // 4) * 8 + zi, lax.rem(y, 4) * 8 + rest)

    def has(j):
        return (gz + j >= 0) & (gz + j < NG)

    def has_slice(k):
        return (zi + k >= 0) & (zi + k < 8)

    def remote(src, dst, send, recv, where):
        return pltpu.make_async_remote_copy(
            src_ref=src, dst_ref=dst, send_sem=send, recv_sem=recv, device_id=where, device_id_type=MESH
        )

    pending = []

    def send(when, *copies):
        @pl.when(when)
        def _():
            for copy in copies:
                copy().start()

        pending.append((when, copies))

    def finish():
        for when, copies in pending:

            @pl.when(when)
            def _(copies=copies):
                for copy in copies:
                    copy().wait_send()

    def tell_one(sem, where):
        pl.semaphore_signal(sem, 1, device_id=where, device_id_type=MESH)

    def tell(sem, dist):
        for j in (-dist, dist):

            @pl.when(has(j))
            def _():
                tell_one(sem, (tm, gz + j))

            @pl.when(has_slice(j))
            def _():
                tell_one(sem, (tm + j, gz))

        tell_one(sem, ygo(dist))
        if dist < 4:
            tell_one(sem, ygo(-dist))

    def hear(sem, dist):
        n = 1 if dist == 4 else 2
        for j in (-dist, dist):
            n = n + has(j).astype(jnp.int32) + has_slice(j).astype(jnp.int32)
        pl.semaphore_wait(sem, n)

    is_b = hi == 1
    is_a = jnp.logical_not(is_b)

    barrier = pltpu.get_barrier_semaphore()
    tell(barrier, 1)
    own_f = pltpu.make_async_copy(starts, fab.at[0, pl.ds(4, 4)], local_sem.at[0])
    own_m = pltpu.make_async_copy(materials, ids.at[pl.ds(4, 4)], local_sem.at[1])
    tables = [
        pltpu.make_async_copy(src, dst, local_sem.at[2 + i])
        for i, (src, dst) in enumerate(((cond_in, cond), (pre_in, pre), (act_in, act)))
    ]
    for table in tables:
        table.start()
    own_m.start()
    own_f.start()

    for j, at in ((-1, 0), (1, 8)):

        @pl.when(jnp.logical_not(has(j)))
        def _():
            fab[0, pl.ds(at, 4)] = jnp.zeros((4, 128, 128), F32)
            ids[pl.ds(at, 4)] = jnp.zeros((4, 128, 128), jnp.int32)
            near[1 + j] = jnp.zeros((2, 8, 128), F32)

    for j in range(-8, 9):

        @pl.when(jnp.logical_not(has(j)))
        def _():
            gbuf[8 + j] = jnp.zeros((3, 8, 128), F32)
            dbuf[8 + j] = jnp.zeros((9, 8, 128), F32)
            c8[8 + j] = jnp.zeros((8, 128), F32)

    for table in tables:
        table.wait()
    c0 = cond[0]
    own_m.wait()
    totals = [jnp.zeros((128, 128), F32) for _ in range(3)]
    for n in range(4):
        layer = ids[4 + n]
        totals = [t + lookup(layer, table) for t, table in zip(totals, (cond, pre, act))]
    own_f.wait()
    totals.append(fab[0, 4] + fab[0, 5] + fab[0, 6] + fab[0, 7])
    pooled = pool(totals, rows4)
    for i in range(3):
        gbuf[8, i] = pooled[i]
    own_coarse = pooled[3]
    near[1, 0] = pooled[0]
    near[1, 1] = own_coarse

    @pl.when(tm == 0)
    def _():
        dbuf[8, 0] = own_coarse
        out[...] = fab[0, pl.ds(4, 4)]

    hear(barrier, 1)

    def near_copy(j):
        side = 0 if j > 0 else 1
        return remote(near.at[1], near.at[1 - j], near_s.at[side], near_r.at[side], (tm, gz + j))

    def slab(j, n, what):
        side = 0 if j > 0 else 1
        here = 3 - n if j > 0 else n
        there = here if j > 0 else 8 + here
        src = (starts if what == 0 else materials).at[here]
        dst = fab.at[0, there] if what == 0 else ids.at[there]
        return remote(src, dst, slab_s.at[side, n, what], slab_r.at[side, n, what], (tm, gz + j))

    for j in (1, -1):
        send(has(j), functools.partial(near_copy, j))
    for n in range(4):
        for j in (1, -1):
            send(has(j), functools.partial(slab, j, n, 1), functools.partial(slab, j, n, 0))
    tell(know.at[0], 1)

    lane = iota((128, 128), 1)
    row = iota((128, 128), 0)
    half = F32(0.5 * STEP)

    def inside_fine(layer):
        return jnp.logical_not(((layer < 4) & (gz == 0)) | ((layer >= 8) & (gz == NG - 1)))

    def sources(layer):
        ident, inside = ids[layer], inside_fine(layer)
        kbuf[layer] = lookup(ident, cond)
        hp[layer] = jnp.where(inside, F32(STEP) * lookup(ident, pre), F32(0.0))
        actb[layer] = lookup(ident, act)

    def faces(layer):
        k = kbuf[layer]
        inside = inside_fine(layer)
        above = half * (k + kbuf[layer + 1])
        below = half * (k + kbuf[layer - 1])
        rest_of = 1.0 - above - below
        for other, edge, ref in (
            (pltpu.roll(k, 127, 1), lane == 127, kxr),
            (pltpu.roll(k, 1, 1), lane == 0, kxl),
            (pltpu.roll(k, 127, 0), row == 127, kyu),
            (pltpu.roll(k, 1, 0), row == 0, kyd),
        ):
            face = half * (k + jnp.where(edge, c0, other))
            rest_of = rest_of - face
            ref[layer] = jnp.where(edge, F32(0.0), face)
        keep[layer] = rest_of
        kz[layer] = jnp.where(inside & inside_fine(layer + 1), above, F32(0.0))
        kz[layer - 1] = jnp.where(inside & inside_fine(layer - 1), below, F32(0.0))

    def fine_step(layer, at):
        v = fab[at, layer]
        new = v * keep[layer] + kz[layer - 1] * fab[at, layer - 1] + kz[layer] * fab[at, layer + 1]
        new = new + kxr[layer] * pltpu.roll(v, 127, 1) + kxl[layer] * pltpu.roll(v, 1, 1)
        new = new + kyu[layer] * pltpu.roll(v, 127, 0) + kyd[layer] * pltpu.roll(v, 1, 0)
        fab[1 - at, layer] = new + release(v, hp[layer], actb[layer])

    def fine_part(layer, inner, below):
        v = fab[0, layer]
        new = v * keep[layer] + kz[below] * fab[0, inner]
        new = new + kxr[layer] * pltpu.roll(v, 127, 1) + kxl[layer] * pltpu.roll(v, 1, 1)
        new = new + kyu[layer] * pltpu.roll(v, 127, 0) + kyd[layer] * pltpu.roll(v, 1, 0)
        fab[1, layer] = new + release(v, hp[layer], actb[layer])

    def slab_here(n, what):
        for j in (1, -1):

            @pl.when(has(-j))
            def _():
                slab(j, n, what).wait_recv()

    def stage(n):
        if n > 0:
            fine_step(5, n % 2)
            fine_step(6, n % 2)
        slab_here(n, 1)
        sources(3 - n)
        sources(8 + n)
        if n == 0:

            def own_faces(i, _):
                faces(4 + i)
                return 0

            lax.fori_loop(0, 4, own_faces, 0)
        else:
            faces(4 - n)
            faces(7 + n)
        low, high = 4 - n, 7 + n
        fine_part(low, low + 1, low)
        fine_part(high, high - 1, high - 1)
        slab_here(n, 0)
        fab[1, low] = fab[1, low] + kz[low - 1] * fab[0, low - 1]
        fab[1, high] = fab[1, high] + kz[high] * fab[0, high + 1]

        def pair(i, _):
            at = lax.rem(i, 2)
            fine_step(4 - n + i, at)
            fine_step(7 + n - i, at)
            return 0

        if n > 0:
            lax.fori_loop(1, n + 1, pair, 0)
        else:
            fine_step(5, 0)
            fine_step(6, 0)

    def own_sources(i, _):
        sources(4 + i)
        return 0

    lax.fori_loop(0, 4, own_sources, 0)
    hear(know.at[0], 1)
    tell(know.at[1], 2)
    for j in (1, -1):

        @pl.when(has(-j))
        def _():
            near_copy(j).wait_recv()

    @pl.when(jnp.logical_not(has(-1)))
    def _():
        near[0, 0] = jnp.full((8, 128), c0, F32)

    @pl.when(jnp.logical_not(has(1)))
    def _():
        near[2, 0] = jnp.full((8, 128), c0, F32)

    sides, vertical, kept, heat = coarse_coefs(
        near[:, 0], gbuf[8, 1][None], c0, [has(-1), has(0), has(1)]
    )
    old = coarse_step(near[:, 1], sides, vertical[:1], vertical[1:], kept, heat, gbuf[8, 2][None])[0]
    oldv[0] = old

    hear(know.at[1], 2)
    tell(know.at[2], 4)
    for n in range(3):
        stage(n)

    def gc_copy(j):
        i = j + 8 if j < 0 else j + 7
        return remote(gbuf.at[8], gbuf.at[8 - j], gc_s.at[i], gc_r.at[i], (tm, gz + j))

    def c0_copy(n):
        return remote(dbuf.at[8, 0], dbuf.at[8, 0], c0_s.at[n - 1], c0_r, (n, gz))

    around = [j for d in range(1, 9) for j in (d, -d)]

    def coarse_out(when):
        @pl.when(when)
        def _():
            hear(know.at[2], 4)
            tell_one(know.at[3], ygo(4))
            tell_one(know.at[3], ring(1))
            tell_one(know.at[3], ring(-1))

        for j in around:
            send(when & (tm != 8) & has(j), functools.partial(gc_copy, j))

    late = zi >= 4
    coarse_out(late)
    stage(3)

    def pass_old():
        return remote(oldv.at[0], oldv.at[1], f_s.at[4], f_r.at[4], (tm + 1, gz))

    def pass_fine(n):
        return remote(fab.at[0, 4 + n], fprev.at[n], f_s.at[n], f_r.at[n], (tm + 1, gz))

    straight = ((2, 72, 56), (3, 72, 56))

    def pass_part(i):
        layer, first, count = straight[i]
        part = pl.ds(first, count)
        return remote(fab.at[0, 4 + layer, part], fprev.at[layer, part], f_s.at[1 + i], part_r.at[4 + i], (8, gz))

    ways = ((1, 0, 128), (2, 0, 72), (3, 0, 72))
    by = (0, 6, 5)

    def to_relay(i):
        layer, first, count = ways[i]
        return remote(
            fab.at[0, 4 + layer, pl.ds(first, count)], relay.at[pl.ds(0, count)], rl_s.at[i], rl_r, (by[i], gz)
        )

    def from_relay(i):
        layer, first, count = ways[i]
        return remote(
            relay.at[pl.ds(0, count)], fprev.at[layer, pl.ds(first, count)], rl_s.at[5], part_r.at[i], (8, gz)
        )

    def relay_on(i):
        @pl.when(tm == by[i])
        def _():
            to_relay(i).wait_recv()

        send(tm == by[i], functools.partial(from_relay, i))

    def c0_here(when):
        @pl.when(when)
        def _():
            c0_copy(1).wait_recv()

    send(tm == 7, *[functools.partial(to_relay, i) for i in range(len(ways))])
    c0_here(tm == 7)
    parts = [functools.partial(pass_part, i) for i in range(len(straight))]
    send(tm == 7, functools.partial(pass_fine, 0), *parts, pass_old)
    ownd[0] = pool([fab[0, 4] + fab[0, 5] + fab[0, 6] + fab[0, 7]], rows4)[0] - old

    eight = tm == 8
    dbuf[8, zi + 1] = ownd[0]

    def dt_copy(k):
        return remote(ownd.at[0], dbuf.at[8, zi + 1], dt_s.at[k - 1], dt_r.at[zi], ring(k))

    def dt_out(when):
        for k in (4, 3, 5, 2, 6, 1, 7):
            to = lax.rem(zi + k, 8)
            skip = is_b & (to == 0)
            send(when(to) & jnp.logical_not(skip), functools.partial(dt_copy, k))

    early = jnp.logical_not(late)
    send(tm == 0, *[functools.partial(c0_copy, n) for n in range(1, 5)])
    dt_out(lambda to: early & (to <= zi + 4))

    coarse_out(early)
    send(tm == 0, *[functools.partial(c0_copy, n) for n in range(5, 8)])
    dt_out(lambda to: late | (to > zi + 4))
    def dt_here(first, end):
        for at in range(first, end):
            go = jnp.logical_not(eight) & (zi != at)

            @pl.when(go)
            def _():
                that = dbuf.at[8, at + 1]
                remote(that, that, dt_s.at[0], dt_r.at[at], ring(1)).wait_recv()

    whole = [pass_old] + [functools.partial(pass_fine, n) for n in range(4)]
    send(zi < 2, *whole)

    def dg_copy(j):
        i = j + 8 if j < 0 else j + 7
        some = pl.ds(0, min(3, 9 - abs(j)))
        return remote(dbuf.at[8, some], dbuf.at[8 - j, some], dg_s.at[i], dg_r.at[i], (tm, gz + j))

    def dm_copy(j):
        i = j + 5 if j < 0 else j + 4
        some = pl.ds(3, min(2, 6 - abs(j)))
        return remote(dbuf.at[8, some], dbuf.at[8 - j, some], dm_s.at[i], dm_r.at[i], (tm, gz + j))

    def dl_copy(j):
        i = j + 3 if j < 0 else j + 2
        some = pl.ds(5, 4 - abs(j))
        return remote(dbuf.at[8, some], dbuf.at[8 - j, some], dl_s.at[i], dl_r.at[i], (tm, gz + j))

    c0_here((tm > 0) & (tm < 7))

    dt_here(0, 2)
    for j in around[::-1]:
        send((tm != 8) & has(j), functools.partial(dg_copy, j))
    dt_here(2, 4)
    for j in around[:10][::-1]:
        send((tm != 8) & has(j), functools.partial(dm_copy, j))
    for i in range(len(ways)):
        relay_on(i)
    dt_here(4, 7)
    relayed = jnp.logical_not(eight)
    for j in around[:6][::-1]:
        send(relayed & has(j), functools.partial(dl_copy, j))
    send((zi >= 2) & (zi < 7), *whole)

    for j in around:

        @pl.when((tm != 8) & has(-j))
        def _():
            gc_copy(j).wait_recv()

    k_all = jnp.concatenate(
        [jnp.where(has(j), gbuf[j + 8 : j + 9, 0], c0) for j in range(-8, 9)], axis=0
    )
    sides, vertical, kept, heat = coarse_coefs(k_all, gbuf[1:16, 1], c0, [has(j) for j in range(-8, 9)])
    for i in range(4):
        cside[i] = sides[i]
    cz[...] = vertical
    ckeep[...] = kept
    chp[...] = heat

    def cr_copy(j):
        return remote(gs.at[9], c8.at[8 - j], cr_s.at[j + 7], cr_r.at[j + 7], (tm + 8, gz + j))

    for j in around:

        @pl.when((tm != 8) & has(-j))
        def _():
            dg_copy(j).wait_recv()

    for j in range(-7, 8):

        @pl.when((tm > 8) & has(-j) & (zi >= abs(j)))
        def _():
            cr_copy(j).wait_recv()

    state[...] = jnp.where(tm > 8, c8[...], dbuf[:, 0])
    for s in range(1, 9):
        if s == 3:
            for j in around[:10]:

                @pl.when((tm != 8) & has(-j))
                def _():
                    dm_copy(j).wait_recv()

        if s == 5:
            for j in around[:6]:

                @pl.when(relayed & has(-j))
                def _():
                    dl_copy(j).wait_recv()

        if s == 8:
            dt_here(7, 8)

        @pl.when((tm < 8) | (zi >= s))
        def _():
            n = 17 - 2 * s
            lo = s - 1
            latest = coarse_step(
                state[pl.ds(lo, n + 2)],
                [cside[i, pl.ds(lo, n)] for i in range(4)],
                cz[pl.ds(lo, n)],
                cz[pl.ds(lo + 1, n)],
                ckeep[pl.ds(lo, n)],
                chp[pl.ds(lo, n)],
                gbuf[pl.ds(s, n), 2],
            )
            gs[s] = latest[8 - s]
            state[pl.ds(s, n)] = latest + dbuf[pl.ds(s, n), s]

    @pl.when(is_a)
    def _():
        gs[9] = state[8]

    def g8_copy():
        return remote(gs.at[8], gs.at[0], cr_s.at[15], cr_r.at[15], (8, gz))

    send(tm == 0, g8_copy)

    pl.semaphore_wait(know.at[3], 3)
    for j in sorted(range(-7, 8), key=lambda j: -abs(j)):
        send((tm > 0) & (tm < 8) & (zi >= abs(j)) & has(j), functools.partial(cr_copy, j))

    @pl.when(eight)
    def _():
        g8_copy().wait_recv()

    @pl.when(tm > 0)
    def _():
        pass_old().wait_recv()
        unpool(gs[zi] - oldv[1], rows4.at[0])

        @pl.when(tm != 8)
        def _():
            for n in range(4):
                pass_fine(n).wait_recv()

        @pl.when(tm == 8)
        def _():
            pass_fine(0).wait_recv()
            for i in range(len(straight)):
                pass_part(i).wait_recv()
            for i in range(len(ways)):
                from_relay(i).wait_recv()

        fine = rows4[0]
        for n in range(4):
            out[n] = fprev[n] + fine

    finish()


def on_device(starts, materials, conductivity, pre_factor, activation):
    vmem, dma = pltpu.VMEM, pltpu.SemaphoreType.DMA
    slabs = vmem((12, 128, 128), F32)
    tile = lambda *lead: vmem(lead + (8, 128), F32)
    held = lambda x: pltpu.with_memory_space_constraint(x, pltpu.HBM)
    result = pl.pallas_call(
        kernel,
        name="parareal",
        out_shape=jax.ShapeDtypeStruct((4, 128, 128), F32),
        in_specs=[pl.BlockSpec(memory_space=pltpu.HBM)] * 5,
        out_specs=pl.BlockSpec(memory_space=pltpu.VMEM),
        scratch_shapes=[
            *([pltpu.SMEM((3,), F32)] * 3),
            vmem((4, 128, 128), F32),
            vmem((2, 12, 128, 128), F32),
            vmem((12, 128, 128), jnp.int32),
            *([slabs] * 9),
            vmem((4, 128, 128), F32),
            vmem((128, 128), F32),
            tile(1),
            tile(2),
            tile(3, 2),
            tile(17, 3),
            tile(17, 9),
            tile(17),
            tile(17),
            tile(10),
            tile(16),
            tile(4, 15),
            tile(15),
            tile(15),
            dma((5,)),
            dma((2,)),
            dma((2,)),
            dma((2, 4, 2)),
            dma((2, 4, 2)),
            dma((8,)),
            dma(()),
            dma((16,)),
            dma((16,)),
            dma((8,)),
            dma((8,)),
            dma((16,)),
            dma((16,)),
            dma((10,)),
            dma((10,)),
            dma((6,)),
            dma((6,)),
            dma((16,)),
            dma((16,)),
            dma((5,)),
            dma((5,)),
            dma((8,)),
            dma((6,)),
            dma(()),
            pltpu.SemaphoreType.REGULAR((4,)),
        ],
        compiler_params=pltpu.CompilerParams(
            collective_id=0, has_side_effects=True, vmem_limit_bytes=40 * 2**20
        ),
        cost_estimate=pl.CostEstimate(flops=50_000_000, bytes_accessed=2_000_000, transcendentals=500_000),
    )(held(starts[0]), held(materials), held(conductivity), held(pre_factor), held(activation))
    return result[None]


def solution(mesh):
    return jax.shard_map(
        on_device,
        mesh=mesh,
        in_specs=(P("tm", "gz", None, None), P("gz", None, None), P(), P(), P()),
        out_specs=P("tm", "gz", None, None),
        check_vma=False,
    )
```
